32 devices in a mesh: fsdp: 16 (over z, x, core), tp: 2 (over y).
Axes of the slice: x: 2, y: 2, z: 4, core: 2. Of those that a mesh axis runs over, the one named last changes fastest.
Arguments:
- grad_kv: bfloat16 [16, 4096, 1024], P('fsdp', None, 'tp'), may hold values from -4 to 4
- grad_gains: bfloat16 [16, 2, 8192], P('fsdp', 'tp'), may hold values from -4 to 4
- kv_weight: float32 [4096, 1024], P('fsdp', 'tp'), may hold values from -0.125 to 0.125
- kv_first: float32 [4096, 1024], P('fsdp', 'tp'), may hold values from -2 to 2
- kv_second: float32 [4096, 1024], P('fsdp', 'tp'), may hold values from 0.004 to 0.4
- gain_weight: float32 [8192], P(('fsdp', 'tp')), may hold values from 0.5 to 1.5
- gain_first: float32 [8192], P(('fsdp', 'tp')), may hold values from -2 to 2
- gain_second: float32 [8192], P(('fsdp', 'tp')), may hold values from 0.05 to 5
- average: bfloat16 [16, 256, 1024], P(None, 'tp'), may hold values from -0.125 to 0.125
Outputs:
- kv_weight_out: float32 [4096, 1024], P('fsdp', 'tp')
- kv_first_out: float32 [4096, 1024], P('fsdp', 'tp')
- kv_second_out: float32 [4096, 1024], P('fsdp', 'tp')
- gain_weight_out: float32 [8192], P(('fsdp', 'tp'))
- gain_first_out: float32 [8192], P(('fsdp', 'tp'))
- gain_second_out: float32 [8192], P(('fsdp', 'tp'))
- kv_blocks: bfloat16 [4096, 1024], P(None, 'tp')
- gain_copy: bfloat16 [8192], replicated
- average_out: bfloat16 [16, 256, 1024], P(None, 'tp')
The draws below stay inside these ranges and needn't reach their ends.
All inputs are finite; a program needn't handle non-finite values.
Results may differ from the reference program's by a relative error of at most 0.003.
Values may be sent and summed in bfloat16 or wider, within the bound.
A program may use at most 64 MiB of HBM per device.

```python
import math
import jax
import jax.numpy as jnp
from jax import lax

D = 4096
STEP = 100
KVW = 1024
PARAMS = 4202496
SHARDS = 16
TPS = 2


def rising_scales(key, count):
    place = jnp.arange(count, dtype=jnp.float32) / count
    spread = jax.random.uniform(key, (count,), jnp.float32)
    return 3.0 ** place * 10.0 ** spread


def draw_grad_kv(key, part):
    keyed = jax.random.fold_in(key, 11)
    k_noise, k_rows, k_cols = jax.random.split(keyed, 3)
    rows = rising_scales(k_rows, D)
    cols = rising_scales(k_cols, KVW)
    base = 3.0 / (41.0 * math.sqrt(SHARDS))
    noise = jnp.clip(jax.random.normal(k_noise, (SHARDS, D, KVW), jnp.float32), -6.0, 6.0)
    values = noise * base * rows[None, :, None] * cols[None, None, :]
    return jnp.clip(values, -4.0, 4.0).astype(jnp.bfloat16)


def draw_grad_gains(key, part):
    keyed = jax.random.fold_in(key, 23)
    k_noise, k_rows = jax.random.split(keyed, 2)
    rows = rising_scales(k_rows, 2 * D)
    base = 2.0 / (8.8 * math.sqrt(SHARDS * TPS))
    noise = jnp.clip(jax.random.normal(k_noise, (SHARDS, TPS, 2 * D), jnp.float32), -6.0, 6.0)
    values = noise * base * rows[None, None, :]
    return jnp.clip(values, -4.0, 4.0).astype(jnp.bfloat16)


def shard_levels(key, shape, pieces, least, top_value):
    level = 1.0
    for axis_at, shards_of in pieces:
        steps = jax.random.uniform(jax.random.fold_in(jax.random.fold_in(key, 6), axis_at), (shards_of,), jnp.float32, least / len(pieces), top_value / len(pieces))
        level = level * jnp.repeat(jnp.exp(steps), shape[axis_at] // shards_of).reshape((-1,) + (1,) * (len(shape) - 1 - axis_at))
    return level


def scatter_about(rng, dims, width, limit, shards=(), kind=jnp.bfloat16):
    gain = shard_levels(rng, dims, shards, -0.22, 0.18) if shards else 1.0
    array = jax.random.normal(rng, dims, jnp.float32) * width * gain
    return jnp.minimum(jnp.maximum(array, -limit), limit).astype(kind)


def setup_inputs(seed: int = 0) -> dict:
    splits = jax.random.split(jax.random.key(seed), 10)
    grad_kv = draw_grad_kv(jax.random.fold_in(splits[9], 71), 0)
    grad_gains = draw_grad_gains(jax.random.fold_in(splits[9], 71), 0)
    kv_weight = scatter_about(splits[2], (D, KVW), 0.02, 0.125, ((0, 16), (1, 2)), jnp.float32)
    kv_first = scatter_about(splits[3], (D, KVW), 0.3, 2.0, ((0, 16), (1, 2)), jnp.float32)
    kv_second = jnp.clip(jnp.exp(math.log(0.4) - 4.6051702 * jax.random.uniform(splits[4], (D, KVW), jnp.float32) ** shard_levels(splits[4], (D, KVW), ((0, 16), (1, 2)), -0.2, 0.2)), 0.004, 0.4)
    gain_weight = jnp.clip(1.0 + 0.1 * jax.random.normal(splits[5], (2 * D,), jnp.float32), 0.5, 1.5)
    gain_first = scatter_about(splits[6], (2 * D,), 0.3, 2.0, ((0, 32),), jnp.float32)
    gain_second = jnp.clip(jnp.exp(math.log(5.0) - 4.6051702 * jax.random.uniform(splits[7], (2 * D,), jnp.float32) ** shard_levels(splits[7], (2 * D,), ((0, 32),), -0.2, 0.2)), 0.05, 5.0)
    average = scatter_about(splits[8], (SHARDS, D // SHARDS, KVW), 0.02, 0.125, ((1, 2),))
    return {"grad_kv": grad_kv, "grad_gains": grad_gains, "kv_weight": kv_weight, "kv_first": kv_first, "kv_second": kv_second, "gain_weight": gain_weight, "gain_first": gain_first, "gain_second": gain_second, "average": average}


def adam_update(grad, first, second, weight, factor, decay):
    clipped = factor * grad
    first_new = 0.9 * first + 0.1 * clipped
    second_new = 0.95 * second + 0.05 * clipped * clipped
    first_fix = 1.0 - 0.9 ** STEP
    second_fix = 1.0 - 0.95 ** STEP
    step_dir = first_new / first_fix / (jnp.sqrt(second_new / second_fix) + 1e-08)
    weight_new = weight - 0.001 * (step_dir + decay * weight)
    return (weight_new, first_new, second_new)

def reference(grad_kv, grad_gains, kv_weight, kv_first, kv_second, gain_weight, gain_first, gain_second, average):
    g_kv = lax.optimization_barrier(jnp.sum(grad_kv, axis=0, dtype=jnp.float32))
    g_gain = lax.optimization_barrier(jnp.sum(grad_gains, axis=(0, 1), dtype=jnp.float32))
    total = jnp.sum(g_kv * g_kv) + jnp.sum(g_gain * g_gain)
    factor = jnp.minimum(jnp.float32(1.0), 1.0 / jnp.sqrt(total / PARAMS + 1e-06))
    kv_w, kv_m, kv_v = adam_update(g_kv, kv_first, kv_second, kv_weight, factor, 0.1)
    gain_w, gain_m, gain_v = adam_update(g_gain, gain_first, gain_second, gain_weight, factor, 0.0)
    kv_blocks = kv_w.astype(jnp.bfloat16)
    gain_copy = gain_w.astype(jnp.bfloat16)
    blended = 0.8 * average.astype(jnp.float32) + 0.2 * kv_blocks.reshape(SHARDS, D // SHARDS, KVW).astype(jnp.float32)
    average_out = blended.astype(jnp.bfloat16)
    return (kv_w, kv_m, kv_v, gain_w, gain_m, gain_v, kv_blocks, gain_copy, average_out)
```

```python
import functools

import jax
import jax.numpy as jnp
from jax import lax
from jax.experimental import pallas as pl
from jax.experimental.pallas import tpu as pltpu
from jax.sharding import PartitionSpec as P

STEP = 100
PARAMS = 4202496
TILE = 32


def adam_update(grad, first, second, weight, factor, decay):
    clipped = factor * grad
    first_new = 0.9 * first + 0.1 * clipped
    second_new = 0.95 * second + 0.05 * clipped * clipped
    first_fix = 1.0 - 0.9**STEP
    second_fix = 1.0 - 0.95**STEP
    step_dir = first_new / first_fix / (jnp.sqrt(second_new / second_fix) + 1e-08)
    weight_new = weight - 0.001 * (step_dir + decay * weight)
    return (weight_new, first_new, second_new)


def step_kernel(
    depth,
    grad,
    gain_grad,
    w_in,
    m_in,
    v_in,
    gw_in,
    gm_in,
    gv_in,
    avg_in,
    w_out,
    m_out,
    v_out,
    gw_out,
    gm_out,
    gv_out,
    kv_out,
    copy_out,
    avg_out,
    own,
    land1,
    send2,
    land2,
    send3,
    land3,
    acc,
    wbuf,
    mbuf,
    vbuf,
    avg,
    kv,
    other,
    gsum,
    gland,
    gz,
    states,
    t1,
    t2,
    own_sem,
    load_sem,
    store_sem,
    p1s,
    p1r,
    p2s,
    p2r,
    p3s,
    p3r,
    gs,
    gr,
    ss,
    sr,
    t1s,
    t1r,
    t2s,
    t2r,
    azs,
    azr,
    axs,
    axr,
    acs,
    acr,
    ays,
    ayr,
    aos,
    aor,
    kvo_sem,
    avo_sem,
):
    f32, bf16 = jnp.float32, jnp.bfloat16
    f = lax.axis_index("fsdp")
    t = lax.axis_index("tp")
    c = lax.rem(f, 2)
    x = lax.rem(lax.div(f, 2), 2)
    z = lax.div(f, 4)
    rows, cols = acc.shape
    half = rows // 2

    def index(zz, xx, cc):
        return (zz * 2 + xx) * 2 + cc

    def flip(bit, by):
        return 1 - bit if by else bit

    def ahead(s):
        return lax.rem(z + s, depth)

    def behind(s):
        return lax.rem(z + depth - s, depth)

    core_peer = (index(z, x, 1 - c), t)
    x_peer = (index(z, 1 - x, c), t)
    y_peer = (f, 1 - t)

    def z_peer(s):
        return (index(ahead(s), x, c), t)

    def near_peer(k):
        return (index(z, flip(x, k // 4), flip(c, (k // 2) % 2)), flip(t, k % 2))

    pending = []

    def push(src, dst, ssem, rsem, to):
        copy = pltpu.make_async_remote_copy(
            src_ref=src,
            dst_ref=dst,
            send_sem=ssem,
            recv_sem=rsem,
            device_id=to,
            device_id_type=pl.DeviceIdType.MESH,
        )
        copy.start()
        pending.append(copy.wait_send)
        return copy

    def local(src, dst, sem):
        copy = pltpu.make_async_copy(src, dst, sem)
        copy.start()
        return copy

    barrier = pltpu.get_barrier_semaphore()
    partners = [near_peer(k) for k in range(1, 8)] + [z_peer(s) for s in range(1, depth)]
    for to in partners:
        pl.semaphore_signal(barrier, inc=1, device_id=to, device_id_type=pl.DeviceIdType.MESH)

    order = [depth // 2] + [s for s in range(1, depth) if s != depth // 2] + [0]
    own_copy, hop1, hop2, hop3 = {}, {}, {}, {}
    for s in order:
        for dx in (1, 0):
            j = s * 2 + dx
            own_copy[j] = local(grad.at[index(ahead(s), flip(x, dx), c)], own.at[j], own_sem.at[j])
    pl.semaphore_wait(barrier, len(partners))

    def piece(h):
        return pl.ds(h * half, half)

    for s in order:
        for dx in (1, 0):
            j = s * 2 + dx
            for h in range(2):
                hop1[j, h] = push(
                    grad.at[index(ahead(s), flip(x, dx), 1 - c), piece(h)],
                    land1.at[j, piece(h)],
                    p1s.at[j, h],
                    p1r.at[j, h],
                    core_peer,
                )
    loads = [
        local(w_in, wbuf, load_sem.at[0]),
        local(m_in, mbuf, load_sem.at[1]),
        local(v_in, vbuf, load_sem.at[2]),
        local(avg_in, avg, load_sem.at[3]),
    ]

    place = f * 2 + t
    gsum[0] = gain_grad[...].astype(f32)
    states[place] = jnp.zeros(states.shape[1:], f32)
    states[place, 0:1, :] = gw_in[...]
    states[place, 1:2, :] = gm_in[...]
    states[place, 2:3, :] = gv_in[...]
    near = [y_peer, core_peer, x_peer]
    gain_hop, state_hop = {}, {}

    def gain_send(stage):
        count = 1 << stage
        span = pl.ds(place - lax.rem(place, count), count)
        if stage < 3:
            gain_hop[stage] = push(
                gsum.at[stage], gland.at[stage], gs.at[stage], gr.at[stage], near[stage]
            )
            state_hop[stage] = push(
                states.at[span], states.at[span], ss.at[stage], sr.at[stage], near[stage]
            )
        else:
            for s in range(1, depth):
                k = 2 + s
                gain_hop[k] = push(gz.at[z], gz.at[z], gs.at[k], gr.at[k], z_peer(s))
                state_hop[k] = push(states.at[span], states.at[span], ss.at[k], sr.at[k], z_peer(s))

    def gain_take(stage):
        gain_hop[stage].wait_recv()
        state_hop[stage].wait_recv()
        total = gsum[stage] + gland[stage]
        if stage < 2:
            gsum[stage + 1] = total
        else:
            gz[z] = total

    gain_send(0)

    def tiles(base, count, body, init=None):
        def step(i, carry):
            return body(pl.ds(pl.multiple_of(base + i * TILE, TILE), TILE), carry)

        return lax.fori_loop(0, count // TILE, step, init)

    for at, s in enumerate(order):
        j = s * 2 + 1
        own_copy[j].wait()
        for h in range(2):
            hop1[j, h].wait_recv()

            def add2(r, carry, j=j, s=s):
                send2[s, r] = (own[j, r].astype(f32) + land1[j, r].astype(f32)).astype(bf16)
                return carry

            tiles(h * half, half, add2, 0)
            hop2[s, h] = push(
                send2.at[s, piece(h)], land2.at[s, piece(h)], p2s.at[s, h], p2r.at[s, h], x_peer
            )

    for at, s in enumerate(order):
        j = s * 2
        own_copy[j].wait()
        for h in range(2):
            hop1[j, h].wait_recv()
            hop2[s, h].wait_recv()

            def add3(r, carry, j=j, s=s):
                value = own[j, r].astype(f32) + land1[j, r].astype(f32) + land2[s, r].astype(f32)
                if s:
                    send3[s - 1, r] = value.astype(bf16)
                else:
                    acc[r] = value
                return carry

            tiles(h * half, half, add3, 0)
            if s:
                hop3[s, h] = push(
                    send3.at[s - 1, piece(h)],
                    land3.at[s - 1, piece(h)],
                    p3s.at[s - 1, h],
                    p3r.at[s - 1, h],
                    z_peer(s),
                )
        if at < 3:
            gain_take(at)
            gain_send(at + 1)

    square = jnp.zeros((8, cols), f32)
    for h in range(2):
        for s in order[:-1]:
            hop3[s, h].wait_recv()

        def add4(r, carry):
            value = acc[r]
            for s in range(1, depth):
                value = value + land3[s - 1, r].astype(f32)
            acc[r] = value
            sq = value * value
            for i in range(TILE // 8):
                carry = carry + sq[i * 8 : i * 8 + 8]
            return carry

        square = tiles(h * half, half, add4, square)
    folded = square[:, 0:128]
    for i in range(1, cols // 128):
        folded = folded + square[:, i * 128 : i * 128 + 128]
    seat = (x * 2 + c) * 2 + t
    t1[seat] = folded
    sums = {}
    for k in range(1, 8):
        sums[k] = push(t1.at[seat], t1.at[seat], t1s.at[k], t1r.at[k], near_peer(k))

    for s in range(1, depth):
        gain_hop[2 + s].wait_recv()
        state_hop[2 + s].wait_recv()
    g_gain = gz[0]
    for i in range(1, depth):
        g_gain = g_gain + gz[i]
    gsum[3] = g_gain

    for copy in loads[:3]:
        copy.wait()
    for k in range(1, 8):
        sums[k].wait_recv()
    t2[z] = jnp.sum(t1[...], axis=0)
    far = {}
    for s in range(1, depth):
        far[s] = push(t2.at[z], t2.at[z], t2s.at[s], t2r.at[s], z_peer(s))
    gain_total = jnp.sum(g_gain * g_gain, keepdims=True)
    for s in range(1, depth):
        far[s].wait_recv()
    total = jnp.sum(jnp.sum(t2[...], axis=0), keepdims=True) + gain_total
    factor = jnp.minimum(f32(1.0), 1.0 / jnp.sqrt(total / PARAMS + 1e-06))

    def update(r, carry):
        new = adam_update(acc[r], mbuf[r], vbuf[r], wbuf[r], factor, 0.1)
        wbuf[r], mbuf[r], vbuf[r] = new
        kv[f, r] = new[0].astype(bf16)
        return carry

    tiles(0, rows, update, 0)

    near_first = [s for s in range(1, depth) if s != depth // 2] + [depth // 2]
    zhop, xhop, chop, yhop, ohop = {}, {}, {}, {}, {}
    for s in near_first:
        zhop[s] = push(kv.at[f], kv.at[f], azs.at[s], azr.at[s], z_peer(s))

    quarter = rows // 2
    give = pl.ds(pl.multiple_of((1 - t) * quarter, quarter), quarter)
    keep = pl.multiple_of(t * quarter, quarter)
    mine = pl.ds(pl.multiple_of(t * cols, cols), cols)
    theirs = pl.ds(pl.multiple_of((1 - t) * cols, cols), cols)
    outs = []

    def spread(s, dx):
        j = s * 2 + dx
        b = index(behind(s), flip(x, dx), c)
        if dx == 0:
            xhop[s] = push(kv.at[b], kv.at[b], axs.at[s], axr.at[s], x_peer)
        yhop[j] = push(kv.at[b, give], other.at[b], ays.at[j], ayr.at[j], y_peer)
        chop[j] = push(kv.at[b], kv.at[b], acs.at[j], acr.at[j], core_peer)
        outs.append(local(kv.at[b], kv_out.at[b], kvo_sem.at[j, 0]))

    def blend(b, sem):
        def body(r, carry):
            source = pl.ds(pl.multiple_of(keep + r.start, TILE), TILE)
            old = avg[b, r, mine].astype(f32)
            avg[b, r, mine] = (0.8 * old + 0.2 * kv[b, source].astype(f32)).astype(bf16)
            old = avg[b, r, theirs].astype(f32)
            avg[b, r, theirs] = (0.8 * old + 0.2 * other[b, r].astype(f32)).astype(bf16)
            return carry

        tiles(0, quarter, body, 0)
        outs.append(local(avg.at[b], avg_out.at[b], sem))

    def finish_here(s, dx):
        j = s * 2 + dx
        b = index(behind(s), flip(x, dx), c)
        yhop[j].wait_recv()
        ohop[j] = push(other.at[b], other.at[b], aos.at[j], aor.at[j], core_peer)
        blend(b, avo_sem.at[j, 0])

    def finish_there(s, dx):
        j = s * 2 + dx
        b = index(behind(s), flip(x, dx), 1 - c)
        chop[j].wait_recv()
        outs.append(local(kv.at[b], kv_out.at[b], kvo_sem.at[j, 1]))
        ohop[j].wait_recv()
        blend(b, avo_sem.at[j, 1])

    events = [(0, 0)]
    last = 0
    for s in near_first:
        events += [(s, 0), (last, 1)]
        last = s
    events.append((last, 1))

    for at, (s, dx) in enumerate(events):
        if dx:
            xhop[s].wait_recv()
        elif s:
            zhop[s].wait_recv()
        spread(s, dx)
        if at == 0:
            outs.append(local(wbuf, w_out, store_sem.at[0]))
            outs.append(local(mbuf, m_out, store_sem.at[1]))
            outs.append(local(vbuf, v_out, store_sem.at[2]))
            fresh = adam_update(
                gsum[3], states[:, 1, :], states[:, 2, :], states[:, 0, :], factor, 0.0
            )
            copy_out[...] = fresh[0].astype(bf16)
            piece_grad = gsum[3, pl.ds(place, 1), :]
            gw_out[...], gm_out[...], gv_out[...] = adam_update(
                piece_grad, gm_in[...], gv_in[...], gw_in[...], factor, 0.0
            )
            loads[3].wait()
        if at >= 2:
            finish_here(*events[at - 2])
        if at >= 3:
            finish_there(*events[at - 3])
    for event in events[-2:]:
        finish_here(*event)
    for event in events[-3:]:
        finish_there(*event)
    for wait in pending:
        wait()
    for copy in outs:
        copy.wait()


def fused_shards(
    grad_kv,
    grad_gains,
    kv_weight,
    kv_first,
    kv_second,
    gain_weight,
    gain_first,
    gain_second,
    average,
):
    n = lax.axis_size("fsdp")
    places = n * lax.axis_size("tp")
    depth = n // 4
    rows, cols = kv_weight.shape
    gain = gain_weight.shape[0]
    f32, bf16 = jnp.float32, jnp.bfloat16
    vmem, hbm = pl.BlockSpec(memory_space=pltpu.VMEM), pl.BlockSpec(memory_space=pl.ANY)
    sems = pltpu.SemaphoreType.DMA
    blocks = 2 * depth
    out_shape = [
        jax.ShapeDtypeStruct((rows, cols), f32),
        jax.ShapeDtypeStruct((rows, cols), f32),
        jax.ShapeDtypeStruct((rows, cols), f32),
        jax.ShapeDtypeStruct((1, gain), f32),
        jax.ShapeDtypeStruct((1, gain), f32),
        jax.ShapeDtypeStruct((1, gain), f32),
        jax.ShapeDtypeStruct((n, rows, cols), bf16),
        jax.ShapeDtypeStruct((places, gain), bf16),
        jax.ShapeDtypeStruct(average.shape, bf16),
    ]
    scratch = [
        pltpu.VMEM((blocks, rows, cols), bf16),
        pltpu.VMEM((blocks, rows, cols), bf16),
        pltpu.VMEM((depth, rows, cols), bf16),
        pltpu.VMEM((depth, rows, cols), bf16),
        pltpu.VMEM((depth - 1, rows, cols), bf16),
        pltpu.VMEM((depth - 1, rows, cols), bf16),
        pltpu.VMEM((rows, cols), f32),
        pltpu.VMEM((rows, cols), f32),
        pltpu.VMEM((rows, cols), f32),
        pltpu.VMEM((rows, cols), f32),
        pltpu.VMEM(average.shape, bf16),
        pltpu.VMEM((n, rows, cols), bf16),
        pltpu.VMEM((n, rows // 2, cols), bf16),
        pltpu.VMEM((4, places, gain), f32),
        pltpu.VMEM((3, places, gain), f32),
        pltpu.VMEM((depth, places, gain), f32),
        pltpu.VMEM((places, 8, gain), f32),
        pltpu.VMEM((8, 8, 128), f32),
        pltpu.VMEM((depth, 8, 128), f32),
        sems((blocks,)),
        sems((4,)),
        sems((3,)),
        sems((blocks, 2)),
        sems((blocks, 2)),
        sems((depth, 2)),
        sems((depth, 2)),
        sems((depth - 1, 2)),
        sems((depth - 1, 2)),
        sems((depth + 2,)),
        sems((depth + 2,)),
        sems((depth + 2,)),
        sems((depth + 2,)),
        sems((8,)),
        sems((8,)),
        sems((depth,)),
        sems((depth,)),
        sems((depth,)),
        sems((depth,)),
        sems((depth,)),
        sems((depth,)),
        sems((blocks,)),
        sems((blocks,)),
        sems((blocks,)),
        sems((blocks,)),
        sems((blocks,)),
        sems((blocks,)),
        sems((blocks, 2)),
        sems((blocks, 2)),
    ]
    w, m, v, gw, gm, gv, kv, copy, avg = pl.pallas_call(
        functools.partial(step_kernel, depth),
        out_shape=out_shape,
        in_specs=[hbm, vmem, hbm, hbm, hbm, vmem, vmem, vmem, hbm],
        out_specs=[hbm, hbm, hbm, vmem, vmem, vmem, hbm, vmem, hbm],
        scratch_shapes=scratch,
        compiler_params=pltpu.CompilerParams(
            collective_id=0, has_side_effects=True, vmem_limit_bytes=48 * 1024 * 1024
        ),
        cost_estimate=pl.CostEstimate(
            flops=40 * n * rows * cols,
            bytes_accessed=20 * n * rows * cols,
            transcendentals=rows * cols,
        ),
    )(
        grad_kv.reshape(n, rows, cols),
        grad_gains.reshape(places, gain),
        kv_weight,
        kv_first,
        kv_second,
        gain_weight.reshape(1, gain),
        gain_first.reshape(1, gain),
        gain_second.reshape(1, gain),
        average,
    )
    return (
        w,
        m,
        v,
        gw.reshape(gain),
        gm.reshape(gain),
        gv.reshape(gain),
        kv.reshape(n * rows, cols),
        copy.reshape(places * gain),
        avg,
    )


def fits(mesh):
    return mesh.shape["tp"] == 2 and mesh.shape["fsdp"] % 4 == 0 and mesh.shape["fsdp"] >= 16


def shards(
    grad_kv,
    grad_gains,
    kv_weight,
    kv_first,
    kv_second,
    gain_weight,
    gain_first,
    gain_second,
    average,
):
    kv_piece = lax.psum_scatter(
        grad_kv[0].astype(jnp.float32), "fsdp", scatter_dimension=0, tiled=True
    )
    kv_square = jnp.sum(kv_piece * kv_piece)
    flat_gain = grad_gains.reshape(-1).astype(jnp.float32)
    gain_piece = lax.psum_scatter(flat_gain, ("fsdp", "tp"), scatter_dimension=0, tiled=True)
    total = lax.psum(kv_square + jnp.sum(gain_piece * gain_piece), ("fsdp", "tp"))
    factor = jnp.minimum(jnp.float32(1.0), 1.0 / jnp.sqrt(total / PARAMS + 1e-06))
    kv_w, kv_m, kv_v = adam_update(kv_piece, kv_first, kv_second, kv_weight, factor, 0.1)
    gain_w, gain_m, gain_v = adam_update(
        gain_piece, gain_first, gain_second, gain_weight, factor, 0.0
    )
    gain_copy = lax.all_gather(gain_w.astype(jnp.bfloat16), ("fsdp", "tp"), axis=0, tiled=True)
    kv_rounded = kv_w.astype(jnp.bfloat16)
    kv_blocks = lax.all_gather(kv_rounded, "fsdp", axis=0, tiled=True)
    shard_count = lax.axis_size("fsdp")
    tp_count = lax.axis_size("tp")
    columns = kv_rounded.shape[1]
    row_count = kv_rounded.shape[0] // tp_count
    moved = lax.all_to_all(
        kv_blocks.reshape(shard_count, tp_count, row_count, columns),
        "tp",
        split_axis=1,
        concat_axis=3,
        tiled=True,
    )
    moved = moved.reshape(shard_count, row_count, columns * tp_count)
    blended = 0.8 * average.astype(jnp.float32) + 0.2 * moved.astype(jnp.float32)
    average_out = blended.astype(jnp.bfloat16)
    return (kv_w, kv_m, kv_v, gain_w, gain_m, gain_v, kv_blocks, gain_copy, average_out)


def solution(mesh):
    in_specs = (
        P("fsdp", None, "tp"),
        P("fsdp", "tp", None),
        P("fsdp", "tp"),
        P("fsdp", "tp"),
        P("fsdp", "tp"),
        P(("fsdp", "tp")),
        P(("fsdp", "tp")),
        P(("fsdp", "tp")),
        P(None, "tp", None),
    )
    out_specs = (
        P("fsdp", "tp"),
        P("fsdp", "tp"),
        P("fsdp", "tp"),
        P(("fsdp", "tp")),
        P(("fsdp", "tp")),
        P(("fsdp", "tp")),
        P(None, "tp"),
        P(),
        P(None, "tp", None),
    )
    body = fused_shards if fits(mesh) else shards
    return jax.shard_map(body, mesh=mesh, in_specs=in_specs, out_specs=out_specs, check_vma=False)
```

```python
import functools

import jax
import jax.numpy as jnp
from jax import lax
from jax.experimental import pallas as pl
from jax.experimental.pallas import tpu as pltpu
from jax.sharding import PartitionSpec as P

STEP = 100
PARAMS = 4202496
TILE = 32


def adam_update(grad, first, second, weight, factor, decay):
    clipped = factor * grad
    first_new = 0.9 * first + 0.1 * clipped
    second_new = 0.95 * second + 0.05 * clipped * clipped
    first_fix = 1.0 - 0.9**STEP
    second_fix = 1.0 - 0.95**STEP
    step_dir = first_new / first_fix / (jnp.sqrt(second_new / second_fix) + 1e-08)
    weight_new = weight - 0.001 * (step_dir + decay * weight)
    return (weight_new, first_new, second_new)


def step_kernel(
    depth,
    grad,
    gain_grad,
    w_in,
    m_in,
    v_in,
    gain_in,
    avg_in,
    wbuf,
    mbuf,
    vbuf,
    gw_out,
    gm_out,
    gv_out,
    kv,
    copy_out,
    avg,
    own,
    land1,
    send2,
    land2,
    send3,
    land3,
    acc,
    other,
    gsum,
    gland,
    gz,
    states,
    t1,
    t2,
    own_sem,
    load_sem,
    p1s,
    p1r,
    p2s,
    p2r,
    p3s,
    p3r,
    gs,
    gr,
    ss,
    sr,
    t1s,
    t1r,
    t2s,
    t2r,
    azs,
    azr,
    axs,
    axr,
    acs,
    acr,
    ays,
    ayr,
    aos,
    aor,
):
    f32, bf16 = jnp.float32, jnp.bfloat16
    f = lax.axis_index("fsdp")
    t = lax.axis_index("tp")
    c = lax.rem(f, 2)
    x = lax.rem(lax.div(f, 2), 2)
    z = lax.div(f, 4)
    rows, cols = acc.shape
    half = rows // 2

    def index(zz, xx, cc):
        return (zz * 2 + xx) * 2 + cc

    def flip(bit, by):
        return 1 - bit if by else bit

    def ahead(s):
        return lax.rem(z + s, depth)

    def behind(s):
        return lax.rem(z + depth - s, depth)

    core_peer = (index(z, x, 1 - c), t)
    x_peer = (index(z, 1 - x, c), t)
    y_peer = (f, 1 - t)

    def z_peer(s):
        return (index(ahead(s), x, c), t)

    def near_peer(k):
        return (index(z, flip(x, k // 4), flip(c, (k // 2) % 2)), flip(t, k % 2))

    pending = []

    def push(src, dst, ssem, rsem, to):
        copy = pltpu.make_async_remote_copy(
            src_ref=src,
            dst_ref=dst,
            send_sem=ssem,
            recv_sem=rsem,
            device_id=to,
            device_id_type=pl.DeviceIdType.MESH,
        )
        copy.start()
        pending.append(copy.wait_send)
        return copy

    def local(src, dst, sem):
        copy = pltpu.make_async_copy(src, dst, sem)
        copy.start()
        return copy

    barrier = pltpu.get_barrier_semaphore()
    partners = [near_peer(k) for k in range(1, 8)] + [z_peer(s) for s in range(1, depth)]
    for to in partners:
        pl.semaphore_signal(barrier, inc=1, device_id=to, device_id_type=pl.DeviceIdType.MESH)

    order = [depth // 2] + [s for s in range(1, depth) if s != depth // 2] + [0]
    own_copy, hop1, hop2, hop3 = {}, {}, {}, {}
    for s in order:
        for dx in (1, 0):
            j = s * 2 + dx
            own_copy[j] = local(grad.at[index(ahead(s), flip(x, dx), c)], own.at[j], own_sem.at[j])
    pl.semaphore_wait(barrier, len(partners))

    def piece(h):
        return pl.ds(h * half, half)

    chunks = [(s, h) for s in order for h in range(2)]
    count = len(chunks)
    first_hops = []
    for i in range(count + 2):
        if i < count:
            first_hops.append((*chunks[i], 1))
        if i >= 2:
            first_hops.append((*chunks[i - 2], 0))

    def push_first(many):
        for s, h, dx in first_hops[:many]:
            j = s * 2 + dx
            hop1[j, h] = push(
                grad.at[index(ahead(s), flip(x, dx), 1 - c), piece(h)],
                land1.at[j, piece(h)],
                p1s.at[j, h],
                p1r.at[j, h],
                core_peer,
            )
        del first_hops[:many]

    push_first(4)

    place = f * 2 + t
    gsum[0] = gain_grad[...].astype(f32)
    states[place] = jnp.zeros(states.shape[1:], f32)
    states[place, 0:3, :] = gain_in[...]
    near = [y_peer, core_peer, x_peer]
    gain_hop, state_hop = {}, {}

    def gain_send(stage):
        count = 1 << stage
        span = pl.ds(place - lax.rem(place, count), count)
        if stage < 3:
            gain_hop[stage] = push(
                gsum.at[stage], gland.at[stage], gs.at[stage], gr.at[stage], near[stage]
            )
            state_hop[stage] = push(
                states.at[span], states.at[span], ss.at[stage], sr.at[stage], near[stage]
            )
        else:
            for s in range(1, depth):
                k = 2 + s
                gain_hop[k] = push(gz.at[z], gz.at[z], gs.at[k], gr.at[k], z_peer(s))
                state_hop[k] = push(states.at[span], states.at[span], ss.at[k], sr.at[k], z_peer(s))

    def gain_take(stage):
        gain_hop[stage].wait_recv()
        state_hop[stage].wait_recv()
        total = gsum[stage] + gland[stage]
        if stage < 2:
            gsum[stage + 1] = total
        else:
            gz[z] = total

    gain_send(0)

    def tiles(base, count, body, init=None):
        def step(i, carry):
            return body(pl.ds(pl.multiple_of(base + i * TILE, TILE), TILE), carry)

        return lax.fori_loop(0, count // TILE, step, init)

    def relay_x(s, h):
        j = s * 2 + 1
        if h == 0:
            own_copy[j].wait()
        hop1[j, h].wait_recv()

        def add2(r, carry):
            send2[s, r] = (own[j, r].astype(f32) + land1[j, r].astype(f32)).astype(bf16)
            return carry

        tiles(h * half, half, add2, 0)
        hop2[s, h] = push(
            send2.at[s, piece(h)], land2.at[s, piece(h)], p2s.at[s, h], p2r.at[s, h], x_peer
        )

    def relay_z(s, h):
        j = s * 2
        if h == 0:
            own_copy[j].wait()
        hop1[j, h].wait_recv()
        hop2[s, h].wait_recv()

        def add3(r, carry):
            value = own[j, r].astype(f32) + land1[j, r].astype(f32) + land2[s, r].astype(f32)
            if s:
                send3[s - 1, r] = value.astype(bf16)
            else:
                acc[r] = value
            return carry

        tiles(h * half, half, add3, 0)
        if s:
            hop3[s, h] = push(
                send3.at[s - 1, piece(h)],
                land3.at[s - 1, piece(h)],
                p3s.at[s - 1, h],
                p3r.at[s - 1, h],
                z_peer(s),
            )

    for i in range(count + 2):
        if i < count:
            relay_x(*chunks[i])
        push_first(2)
        if i == 1:
            loads = [
                local(w_in, wbuf, load_sem.at[0]),
                local(m_in, mbuf, load_sem.at[1]),
                local(v_in, vbuf, load_sem.at[2]),
                local(avg_in, avg, load_sem.at[3]),
            ]
        if i >= 2:
            relay_z(*chunks[i - 2])
        if i in (1, 3, 5):
            gain_take(i // 2)
            gain_send(i // 2 + 1)

    square = jnp.zeros((8, cols), f32)
    for h in range(2):
        for s in order[:-1]:
            hop3[s, h].wait_recv()

        def add4(r, carry):
            value = acc[r]
            for s in range(1, depth):
                value = value + land3[s - 1, r].astype(f32)
            acc[r] = value
            sq = value * value
            for i in range(TILE // 8):
                carry = carry + sq[i * 8 : i * 8 + 8]
            return carry

        square = tiles(h * half, half, add4, square)
    folded = square[:, 0:128]
    for i in range(1, cols // 128):
        folded = folded + square[:, i * 128 : i * 128 + 128]
    seat = (x * 2 + c) * 2 + t
    t1[seat] = folded
    sums = {}
    for k in range(1, 8):
        sums[k] = push(t1.at[seat], t1.at[seat], t1s.at[k], t1r.at[k], near_peer(k))

    for s in range(1, depth):
        gain_hop[2 + s].wait_recv()
        state_hop[2 + s].wait_recv()
    g_gain = gz[0]
    for i in range(1, depth):
        g_gain = g_gain + gz[i]
    gsum[3] = g_gain

    for copy in loads[:3]:
        copy.wait()
    for k in range(1, 8):
        sums[k].wait_recv()
    t2[z] = jnp.sum(t1[...], axis=0)
    far = {}
    for s in range(1, depth):
        far[s] = push(t2.at[z], t2.at[z], t2s.at[s], t2r.at[s], z_peer(s))
    gain_total = jnp.sum(g_gain * g_gain, keepdims=True)
    for s in range(1, depth):
        far[s].wait_recv()
    total = jnp.sum(jnp.sum(t2[...], axis=0), keepdims=True) + gain_total
    factor = jnp.minimum(f32(1.0), 1.0 / jnp.sqrt(total / PARAMS + 1e-06))

    def update(r, carry):
        new = adam_update(acc[r], mbuf[r], vbuf[r], wbuf[r], factor, 0.1)
        wbuf[r], mbuf[r], vbuf[r] = new
        kv[f, r] = new[0].astype(bf16)
        return carry

    tiles(0, rows, update, 0)

    quarter = rows // 2
    keep = pl.multiple_of(t * quarter, quarter)
    spans = [
        pl.ds(pl.multiple_of((1 - t) * quarter, quarter), quarter),
        pl.ds(keep, quarter),
    ]
    mine = pl.ds(pl.multiple_of(t * cols, cols), cols)
    theirs = pl.ds(pl.multiple_of((1 - t) * cols, cols), cols)
    near_first = [s for s in range(1, depth) if s != depth // 2] + [depth // 2]
    zlist = [(s, h) for s in near_first for h in range(2)]
    xlist = [(0, 0), (0, 1)] + zlist
    zhop, xhop, chop, yhop, ohop = {}, {}, {}, {}, {}

    def push_z(many):
        for s, h in zlist[:many]:
            part = kv.at[f, spans[h]]
            zhop[s, h] = push(part, part, azs.at[s, h], azr.at[s, h], z_peer(s))
        del zlist[:many]

    def spread(s, dx, h):
        j = s * 2 + dx
        b = index(behind(s), flip(x, dx), c)
        part = kv.at[b, spans[h]]
        if dx == 0:
            xhop[s, h] = push(part, part, axs.at[s, h], axr.at[s, h], x_peer)
        if h == 0:
            yhop[j] = push(part, other.at[b], ays.at[j], ayr.at[j], y_peer)
        chop[j, h] = push(part, part, acs.at[j, h], acr.at[j, h], core_peer)

    def blend(b):
        def body(r, carry):
            source = pl.ds(pl.multiple_of(keep + r.start, TILE), TILE)
            old = avg[b, r, mine].astype(f32)
            avg[b, r, mine] = (0.8 * old + 0.2 * kv[b, source].astype(f32)).astype(bf16)
            old = avg[b, r, theirs].astype(f32)
            avg[b, r, theirs] = (0.8 * old + 0.2 * other[b, r].astype(f32)).astype(bf16)
            return carry

        tiles(0, quarter, body, 0)

    def finish_here(s, dx):
        j = s * 2 + dx
        b = index(behind(s), flip(x, dx), c)
        yhop[j].wait_recv()
        ohop[j] = push(other.at[b], other.at[b], aos.at[j], aor.at[j], core_peer)
        blend(b)

    def finish_there(s, dx):
        j = s * 2 + dx
        b = index(behind(s), flip(x, dx), 1 - c)
        for h in range(2):
            chop[j, h].wait_recv()
        ohop[j].wait_recv()
        blend(b)

    push_z(2)
    here, there = [], []
    for i in range(len(xlist) + 5):
        if i < len(xlist):
            s, h = xlist[i]
            if s:
                zhop[s, h].wait_recv()
                push_z(1)
            spread(s, 0, h)
            if h:
                here.append((i + 2, s, 0))
        if 2 <= i < len(xlist) + 2:
            s, h = xlist[i - 2]
            xhop[s, h].wait_recv()
            spread(s, 1, h)
            if h:
                here.append((i + 1, s, 1))
        if i == 0:
            fresh = adam_update(
                gsum[3], states[:, 1, :], states[:, 2, :], states[:, 0, :], factor, 0.0
            )
            copy_out[...] = fresh[0].astype(bf16)
            piece_grad = gsum[3, pl.ds(place, 1), :]
            gw_out[...], gm_out[...], gv_out[...] = adam_update(
                piece_grad, gain_in[1:2], gain_in[2:3], gain_in[0:1], factor, 0.0
            )
            loads[3].wait()
        for due, s, dx in here:
            if due == i:
                finish_here(s, dx)
                there.append((i + 1, s, dx))
        for due, s, dx in there:
            if due == i:
                finish_there(s, dx)
    for wait in pending:
        wait()


def store_kernel(*refs):
    count = len(refs) // 2
    sources, targets, sem = refs[:count], refs[count:-1], refs[-1]
    copies = []
    for at, (src, dst) in enumerate(zip(sources, targets)):
        parts = 4 if src.ndim == 3 else 1
        step = src.shape[0] // parts
        for part in range(parts):
            span = pl.ds(part * step, step)
            copy = pltpu.make_async_copy(src.at[span], dst.at[span], sem.at[at, part])
            copy.start()
            copies.append(copy)
    for copy in copies:
        copy.wait()


def fused_shards(
    grad_kv,
    grad_gains,
    kv_weight,
    kv_first,
    kv_second,
    gain_weight,
    gain_first,
    gain_second,
    average,
):
    n = lax.axis_size("fsdp")
    places = n * lax.axis_size("tp")
    depth = n // 4
    rows, cols = kv_weight.shape
    gain = gain_weight.shape[0]
    f32, bf16 = jnp.float32, jnp.bfloat16
    vmem, hbm = pl.BlockSpec(memory_space=pltpu.VMEM), pl.BlockSpec(memory_space=pltpu.HBM)
    sems = pltpu.SemaphoreType.DMA
    blocks = 2 * depth
    out_shape = [
        jax.ShapeDtypeStruct((rows, cols), f32),
        jax.ShapeDtypeStruct((rows, cols), f32),
        jax.ShapeDtypeStruct((rows, cols), f32),
        jax.ShapeDtypeStruct((1, gain), f32),
        jax.ShapeDtypeStruct((1, gain), f32),
        jax.ShapeDtypeStruct((1, gain), f32),
        jax.ShapeDtypeStruct((n, rows, cols), bf16),
        jax.ShapeDtypeStruct((places, gain), bf16),
        jax.ShapeDtypeStruct(average.shape, bf16),
    ]
    scratch = [
        pltpu.VMEM((blocks, rows, cols), bf16),
        pltpu.VMEM((blocks, rows, cols), bf16),
        pltpu.VMEM((depth, rows, cols), bf16),
        pltpu.VMEM((depth, rows, cols), bf16),
        pltpu.VMEM((depth - 1, rows, cols), bf16),
        pltpu.VMEM((depth - 1, rows, cols), bf16),
        pltpu.VMEM((rows, cols), f32),
        pltpu.VMEM((n, rows // 2, cols), bf16),
        pltpu.VMEM((4, places, gain), f32),
        pltpu.VMEM((3, places, gain), f32),
        pltpu.VMEM((depth, places, gain), f32),
        pltpu.VMEM((places, 8, gain), f32),
        pltpu.VMEM((8, 8, 128), f32),
        pltpu.VMEM((depth, 8, 128), f32),
        sems((blocks,)),
        sems((4,)),
        sems((blocks, 2)),
        sems((blocks, 2)),
        sems((depth, 2)),
        sems((depth, 2)),
        sems((depth - 1, 2)),
        sems((depth - 1, 2)),
        sems((depth + 2,)),
        sems((depth + 2,)),
        sems((depth + 2,)),
        sems((depth + 2,)),
        sems((8,)),
        sems((8,)),
        sems((depth,)),
        sems((depth,)),
        sems((depth, 2)),
        sems((depth, 2)),
        sems((depth, 2)),
        sems((depth, 2)),
        sems((blocks, 2)),
        sems((blocks, 2)),
        sems((blocks,)),
        sems((blocks,)),
        sems((blocks,)),
        sems((blocks,)),
    ]
    held = pl.pallas_call(
        functools.partial(step_kernel, depth),
        out_shape=out_shape,
        in_specs=[hbm, vmem, hbm, hbm, hbm, vmem, hbm],
        out_specs=[vmem] * 9,
        scratch_shapes=scratch,
        compiler_params=pltpu.CompilerParams(
            collective_id=0, has_side_effects=True, vmem_limit_bytes=40 * 1024 * 1024
        ),
        cost_estimate=pl.CostEstimate(
            flops=40 * n * rows * cols,
            bytes_accessed=20 * n * rows * cols,
            transcendentals=rows * cols,
        ),
    )(
        grad_kv.reshape(n, rows, cols),
        grad_gains.reshape(places, gain),
        kv_weight,
        kv_first,
        kv_second,
        jnp.stack([gain_weight, gain_first, gain_second]),
        average,
    )
    w, m, v, gw, gm, gv, kv, copy, avg = pl.pallas_call(
        store_kernel,
        out_shape=out_shape,
        in_specs=[vmem] * 9,
        out_specs=[hbm] * 9,
        scratch_shapes=[sems((9, 4))],
        compiler_params=pltpu.CompilerParams(has_side_effects=True),
    )(*held)
    return (
        w,
        m,
        v,
        gw.reshape(gain),
        gm.reshape(gain),
        gv.reshape(gain),
        kv.reshape(n * rows, cols),
        copy.reshape(places * gain),
        avg,
    )


def fits(mesh):
    return mesh.shape["tp"] == 2 and mesh.shape["fsdp"] % 4 == 0 and mesh.shape["fsdp"] >= 16


def shards(
    grad_kv,
    grad_gains,
    kv_weight,
    kv_first,
    kv_second,
    gain_weight,
    gain_first,
    gain_second,
    average,
):
    kv_piece = lax.psum_scatter(
        grad_kv[0].astype(jnp.float32), "fsdp", scatter_dimension=0, tiled=True
    )
    kv_square = jnp.sum(kv_piece * kv_piece)
    flat_gain = grad_gains.reshape(-1).astype(jnp.float32)
    gain_piece = lax.psum_scatter(flat_gain, ("fsdp", "tp"), scatter_dimension=0, tiled=True)
    total = lax.psum(kv_square + jnp.sum(gain_piece * gain_piece), ("fsdp", "tp"))
    factor = jnp.minimum(jnp.float32(1.0), 1.0 / jnp.sqrt(total / PARAMS + 1e-06))
    kv_w, kv_m, kv_v = adam_update(kv_piece, kv_first, kv_second, kv_weight, factor, 0.1)
    gain_w, gain_m, gain_v = adam_update(
        gain_piece, gain_first, gain_second, gain_weight, factor, 0.0
    )
    gain_copy = lax.all_gather(gain_w.astype(jnp.bfloat16), ("fsdp", "tp"), axis=0, tiled=True)
    kv_rounded = kv_w.astype(jnp.bfloat16)
    kv_blocks = lax.all_gather(kv_rounded, "fsdp", axis=0, tiled=True)
    shard_count = lax.axis_size("fsdp")
    tp_count = lax.axis_size("tp")
    columns = kv_rounded.shape[1]
    row_count = kv_rounded.shape[0] // tp_count
    moved = lax.all_to_all(
        kv_blocks.reshape(shard_count, tp_count, row_count, columns),
        "tp",
        split_axis=1,
        concat_axis=3,
        tiled=True,
    )
    moved = moved.reshape(shard_count, row_count, columns * tp_count)
    blended = 0.8 * average.astype(jnp.float32) + 0.2 * moved.astype(jnp.float32)
    average_out = blended.astype(jnp.bfloat16)
    return (kv_w, kv_m, kv_v, gain_w, gain_m, gain_v, kv_blocks, gain_copy, average_out)


def solution(mesh):
    in_specs = (
        P("fsdp", None, "tp"),
        P("fsdp", "tp", None),
        P("fsdp", "tp"),
        P("fsdp", "tp"),
        P("fsdp", "tp"),
        P(("fsdp", "tp")),
        P(("fsdp", "tp")),
        P(("fsdp", "tp")),
        P(None, "tp", None),
    )
    out_specs = (
        P("fsdp", "tp"),
        P("fsdp", "tp"),
        P("fsdp", "tp"),
        P(("fsdp", "tp")),
        P(("fsdp", "tp")),
        P(("fsdp", "tp")),
        P(None, "tp"),
        P(),
        P(None, "tp", None),
    )
    body = fused_shards if fits(mesh) else shards
    return jax.shard_map(body, mesh=mesh, in_specs=in_specs, out_specs=out_specs, check_vma=False)
```

```python
import functools

import jax
import jax.numpy as jnp
from jax import lax
from jax.experimental import pallas as pl
from jax.experimental.pallas import tpu as pltpu
from jax.sharding import PartitionSpec as P

STEP = 100
PARAMS = 4202496
TILE = 32


def adam_update(grad, first, second, weight, factor, decay):
    clipped = factor * grad
    first_new = 0.9 * first + 0.1 * clipped
    second_new = 0.95 * second + 0.05 * clipped * clipped
    first_fix = 1.0 - 0.9**STEP
    second_fix = 1.0 - 0.95**STEP
    step_dir = first_new / first_fix / (jnp.sqrt(second_new / second_fix) + 1e-08)
    weight_new = weight - 0.001 * (step_dir + decay * weight)
    return (weight_new, first_new, second_new)


def step_kernel(
    depth,
    grad,
    gain_grad,
    w_in,
    m_in,
    v_in,
    gain_in,
    avg_in,
    wbuf,
    mbuf,
    vbuf,
    gw_out,
    gm_out,
    gv_out,
    kv,
    copy_out,
    avg,
    own,
    land1,
    send2,
    land2,
    send3,
    land3,
    acc,
    other,
    gsum,
    gland,
    gz,
    states,
    t1,
    t2,
    own_sem,
    load_sem,
    p1s,
    p1r,
    p2s,
    p2r,
    p3s,
    p3r,
    gs,
    gr,
    ss,
    sr,
    t1s,
    t1r,
    t2s,
    t2r,
    azs,
    azr,
    axs,
    axr,
    acs,
    acr,
    ays,
    ayr,
    aos,
    aor,
):
    f32, bf16 = jnp.float32, jnp.bfloat16
    f = lax.axis_index("fsdp")
    t = lax.axis_index("tp")
    c = lax.rem(f, 2)
    x = lax.rem(lax.div(f, 2), 2)
    z = lax.div(f, 4)
    rows, cols = acc.shape
    half = rows // 2

    def index(zz, xx, cc):
        return (zz * 2 + xx) * 2 + cc

    def flip(bit, by):
        return 1 - bit if by else bit

    def ahead(s):
        return lax.rem(z + s, depth)

    def behind(s):
        return lax.rem(z + depth - s, depth)

    core_peer = (index(z, x, 1 - c), t)
    x_peer = (index(z, 1 - x, c), t)
    y_peer = (f, 1 - t)

    def z_peer(s):
        return (index(ahead(s), x, c), t)

    def near_peer(k):
        return (index(z, flip(x, k // 4), flip(c, (k // 2) % 2)), flip(t, k % 2))

    pending = []

    def push(src, dst, ssem, rsem, to):
        copy = pltpu.make_async_remote_copy(
            src_ref=src,
            dst_ref=dst,
            send_sem=ssem,
            recv_sem=rsem,
            device_id=to,
            device_id_type=pl.DeviceIdType.MESH,
        )
        copy.start()
        pending.append(copy.wait_send)
        return copy

    def local(src, dst, sem):
        copy = pltpu.make_async_copy(src, dst, sem)
        copy.start()
        return copy

    barrier = pltpu.get_barrier_semaphore()
    partners = [near_peer(k) for k in range(1, 8)] + [z_peer(s) for s in range(1, depth)]
    for to in partners:
        pl.semaphore_signal(barrier, inc=1, device_id=to, device_id_type=pl.DeviceIdType.MESH)

    order = [depth // 2] + [s for s in range(1, depth) if s != depth // 2] + [0]
    own_copy, hop1, hop2, hop3 = {}, {}, {}, {}
    for s in order:
        for dx in (1, 0):
            j = s * 2 + dx
            own_copy[j] = local(grad.at[index(ahead(s), flip(x, dx), c)], own.at[j], own_sem.at[j])
    pl.semaphore_wait(barrier, len(partners))

    def piece(h):
        return pl.ds(h * half, half)

    chunks = [(s, h) for s in order for h in range(2)]
    count = len(chunks)
    first_hops = []
    for i in range(count + 2):
        if i < count:
            first_hops.append((*chunks[i], 1))
        if i >= 2:
            first_hops.append((*chunks[i - 2], 0))

    def push_first(many):
        for s, h, dx in first_hops[:many]:
            j = s * 2 + dx
            hop1[j, h] = push(
                grad.at[index(ahead(s), flip(x, dx), 1 - c), piece(h)],
                land1.at[j, piece(h)],
                p1s.at[j, h],
                p1r.at[j, h],
                core_peer,
            )
        del first_hops[:many]

    push_first(4)

    place = f * 2 + t
    gsum[0] = gain_grad[...].astype(f32)
    states[place] = jnp.zeros(states.shape[1:], f32)
    states[place, 0:3, :] = gain_in[...]
    near = [y_peer, core_peer, x_peer]
    gain_hop, state_hop = {}, {}

    def gain_send(stage):
        count = 1 << stage
        span = pl.ds(place - lax.rem(place, count), count)
        if stage < 3:
            gain_hop[stage] = push(
                gsum.at[stage], gland.at[stage], gs.at[stage], gr.at[stage], near[stage]
            )
            state_hop[stage] = push(
                states.at[span], states.at[span], ss.at[stage], sr.at[stage], near[stage]
            )
        else:
            for s in range(1, depth):
                k = 2 + s
                gain_hop[k] = push(gz.at[z], gz.at[z], gs.at[k], gr.at[k], z_peer(s))
                state_hop[k] = push(states.at[span], states.at[span], ss.at[k], sr.at[k], z_peer(s))

    def gain_take(stage):
        gain_hop[stage].wait_recv()
        state_hop[stage].wait_recv()
        total = gsum[stage] + gland[stage]
        if stage < 2:
            gsum[stage + 1] = total
        else:
            gz[z] = total

    gain_send(0)

    def tiles(base, count, body, init=None):
        def step(i, carry):
            return body(pl.ds(pl.multiple_of(base + i * TILE, TILE), TILE), carry)

        return lax.fori_loop(0, count // TILE, step, init)

    def relay_x(s, h):
        j = s * 2 + 1
        if h == 0:
            own_copy[j].wait()
        hop1[j, h].wait_recv()

        def add2(r, carry):
            send2[s, r] = (own[j, r].astype(f32) + land1[j, r].astype(f32)).astype(bf16)
            return carry

        tiles(h * half, half, add2, 0)
        hop2[s, h] = push(
            send2.at[s, piece(h)], land2.at[s, piece(h)], p2s.at[s, h], p2r.at[s, h], x_peer
        )

    def relay_z(s, h):
        j = s * 2
        if h == 0:
            own_copy[j].wait()
        hop1[j, h].wait_recv()
        hop2[s, h].wait_recv()

        def add3(r, carry):
            value = own[j, r].astype(f32) + land1[j, r].astype(f32) + land2[s, r].astype(f32)
            if s:
                send3[s - 1, r] = value.astype(bf16)
            else:
                acc[r] = value
            return carry

        tiles(h * half, half, add3, 0)
        if s:
            hop3[s, h] = push(
                send3.at[s - 1, piece(h)],
                land3.at[s - 1, piece(h)],
                p3s.at[s - 1, h],
                p3r.at[s - 1, h],
                z_peer(s),
            )

    for i in range(count + 2):
        if i < count:
            relay_x(*chunks[i])
        push_first(2)
        if i == 1:
            loads = [
                local(w_in, wbuf, load_sem.at[0]),
                local(m_in, mbuf, load_sem.at[1]),
                local(v_in, vbuf, load_sem.at[2]),
                local(avg_in, avg, load_sem.at[3]),
            ]
        if i >= 2:
            relay_z(*chunks[i - 2])
        if i in (1, 3, 5):
            gain_take(i // 2)
            gain_send(i // 2 + 1)

    square = jnp.zeros((8, cols), f32)
    for h in range(2):
        for s in order[:-1]:
            hop3[s, h].wait_recv()

        def add4(r, carry):
            value = acc[r]
            for s in range(1, depth):
                value = value + land3[s - 1, r].astype(f32)
            acc[r] = value
            sq = value * value
            for i in range(TILE // 8):
                carry = carry + sq[i * 8 : i * 8 + 8]
            return carry

        square = tiles(h * half, half, add4, square)
    folded = square[:, 0:128]
    for i in range(1, cols // 128):
        folded = folded + square[:, i * 128 : i * 128 + 128]
    seat = (x * 2 + c) * 2 + t
    t1[seat] = folded
    sums = {}
    for k in range(1, 8):
        sums[k] = push(t1.at[seat], t1.at[seat], t1s.at[k], t1r.at[k], near_peer(k))

    for s in range(1, depth):
        gain_hop[2 + s].wait_recv()
        state_hop[2 + s].wait_recv()
    g_gain = gz[0]
    for i in range(1, depth):
        g_gain = g_gain + gz[i]
    gsum[3] = g_gain

    for copy in loads[:3]:
        copy.wait()
    for k in range(1, 8):
        sums[k].wait_recv()
    t2[z] = jnp.sum(t1[...], axis=0)
    far = {}
    for s in range(1, depth):
        far[s] = push(t2.at[z], t2.at[z], t2s.at[s], t2r.at[s], z_peer(s))
    gain_total = jnp.sum(g_gain * g_gain, keepdims=True)
    for s in range(1, depth):
        far[s].wait_recv()
    total = jnp.sum(jnp.sum(t2[...], axis=0), keepdims=True) + gain_total
    factor = jnp.minimum(f32(1.0), 1.0 / jnp.sqrt(total / PARAMS + 1e-06))

    def update(r, carry):
        new = adam_update(acc[r], mbuf[r], vbuf[r], wbuf[r], factor, 0.1)
        wbuf[r], mbuf[r], vbuf[r] = new
        kv[f, r] = new[0].astype(bf16)
        return carry


    quarter = rows // 2
    keep = pl.multiple_of(t * quarter, quarter)
    spans = [
        pl.ds(pl.multiple_of((1 - t) * quarter, quarter), quarter),
        pl.ds(keep, quarter),
    ]
    mine = pl.ds(pl.multiple_of(t * cols, cols), cols)
    theirs = pl.ds(pl.multiple_of((1 - t) * cols, cols), cols)
    near_first = [s for s in range(1, depth) if s != depth // 2] + [depth // 2]
    zlist = [(s, h) for s in near_first for h in range(2)]
    xlist = [(0, 0), (0, 1)] + zlist
    zhop, xhop, chop, yhop, ohop = {}, {}, {}, {}, {}

    def push_z(many):
        for s, h in zlist[:many]:
            part = kv.at[f, spans[h]]
            zhop[s, h] = push(part, part, azs.at[s, h], azr.at[s, h], z_peer(s))
        del zlist[:many]

    def spread(s, dx, h):
        j = s * 2 + dx
        b = index(behind(s), flip(x, dx), c)
        part = kv.at[b, spans[h]]
        if dx == 0:
            xhop[s, h] = push(part, part, axs.at[s, h], axr.at[s, h], x_peer)
        if h == 0:
            yhop[j] = push(part, other.at[b], ays.at[j], ayr.at[j], y_peer)
        chop[j, h] = push(part, part, acs.at[j, h], acr.at[j, h], core_peer)

    def blend(b):
        def body(r, carry):
            source = pl.ds(pl.multiple_of(keep + r.start, TILE), TILE)
            old = avg[b, r, mine].astype(f32)
            avg[b, r, mine] = (0.8 * old + 0.2 * kv[b, source].astype(f32)).astype(bf16)
            old = avg[b, r, theirs].astype(f32)
            avg[b, r, theirs] = (0.8 * old + 0.2 * other[b, r].astype(f32)).astype(bf16)
            return carry

        tiles(0, quarter, body, 0)

    def finish_here(s, dx):
        j = s * 2 + dx
        b = index(behind(s), flip(x, dx), c)
        yhop[j].wait_recv()
        ohop[j] = push(other.at[b], other.at[b], aos.at[j], aor.at[j], core_peer)
        blend(b)

    def finish_there(s, dx):
        j = s * 2 + dx
        b = index(behind(s), flip(x, dx), 1 - c)
        for h in range(2):
            chop[j, h].wait_recv()
        ohop[j].wait_recv()
        blend(b)

    here, there = [], []
    for i in range(len(xlist) + 5):
        if i < len(xlist):
            s, h = xlist[i]
            if s:
                zhop[s, h].wait_recv()
                push_z(1)
            else:
                tiles(pl.multiple_of((1 - t if h == 0 else t) * quarter, quarter), quarter, update, 0)
                push_z(1)
            spread(s, 0, h)
            if h:
                here.append((i + 2, s, 0))
        if 2 <= i < len(xlist) + 2:
            s, h = xlist[i - 2]
            xhop[s, h].wait_recv()
            spread(s, 1, h)
            if h:
                here.append((i + 1, s, 1))
        if i == 0:
            fresh = adam_update(
                gsum[3], states[:, 1, :], states[:, 2, :], states[:, 0, :], factor, 0.0
            )
            copy_out[...] = fresh[0].astype(bf16)
            piece_grad = gsum[3, pl.ds(place, 1), :]
            gw_out[...], gm_out[...], gv_out[...] = adam_update(
                piece_grad, gain_in[1:2], gain_in[2:3], gain_in[0:1], factor, 0.0
            )
            loads[3].wait()
        for due, s, dx in here:
            if due == i:
                finish_here(s, dx)
                there.append((i + 1, s, dx))
        for due, s, dx in there:
            if due == i:
                finish_there(s, dx)
    for wait in pending:
        wait()


def store_kernel(*refs):
    count = len(refs) // 2
    sources, targets, sem = refs[:count], refs[count:-1], refs[-1]
    copies = []
    for at, (src, dst) in enumerate(zip(sources, targets)):
        parts = 4 if src.ndim == 3 else 1
        step = src.shape[0] // parts
        for part in range(parts):
            span = pl.ds(part * step, step)
            copy = pltpu.make_async_copy(src.at[span], dst.at[span], sem.at[at, part])
            copy.start()
            copies.append(copy)
    for copy in copies:
        copy.wait()


def fused_shards(
    grad_kv,
    grad_gains,
    kv_weight,
    kv_first,
    kv_second,
    gain_weight,
    gain_first,
    gain_second,
    average,
):
    n = lax.axis_size("fsdp")
    places = n * lax.axis_size("tp")
    depth = n // 4
    rows, cols = kv_weight.shape
    gain = gain_weight.shape[0]
    f32, bf16 = jnp.float32, jnp.bfloat16
    vmem, hbm = pl.BlockSpec(memory_space=pltpu.VMEM), pl.BlockSpec(memory_space=pltpu.HBM)
    sems = pltpu.SemaphoreType.DMA
    blocks = 2 * depth
    out_shape = [
        jax.ShapeDtypeStruct((rows, cols), f32),
        jax.ShapeDtypeStruct((rows, cols), f32),
        jax.ShapeDtypeStruct((rows, cols), f32),
        jax.ShapeDtypeStruct((1, gain), f32),
        jax.ShapeDtypeStruct((1, gain), f32),
        jax.ShapeDtypeStruct((1, gain), f32),
        jax.ShapeDtypeStruct((n, rows, cols), bf16),
        jax.ShapeDtypeStruct((places, gain), bf16),
        jax.ShapeDtypeStruct(average.shape, bf16),
    ]
    scratch = [
        pltpu.VMEM((blocks, rows, cols), bf16),
        pltpu.VMEM((blocks, rows, cols), bf16),
        pltpu.VMEM((depth, rows, cols), bf16),
        pltpu.VMEM((depth, rows, cols), bf16),
        pltpu.VMEM((depth - 1, rows, cols), bf16),
        pltpu.VMEM((depth - 1, rows, cols), bf16),
        pltpu.VMEM((rows, cols), f32),
        pltpu.VMEM((n, rows // 2, cols), bf16),
        pltpu.VMEM((4, places, gain), f32),
        pltpu.VMEM((3, places, gain), f32),
        pltpu.VMEM((depth, places, gain), f32),
        pltpu.VMEM((places, 8, gain), f32),
        pltpu.VMEM((8, 8, 128), f32),
        pltpu.VMEM((depth, 8, 128), f32),
        sems((blocks,)),
        sems((4,)),
        sems((blocks, 2)),
        sems((blocks, 2)),
        sems((depth, 2)),
        sems((depth, 2)),
        sems((depth - 1, 2)),
        sems((depth - 1, 2)),
        sems((depth + 2,)),
        sems((depth + 2,)),
        sems((depth + 2,)),
        sems((depth + 2,)),
        sems((8,)),
        sems((8,)),
        sems((depth,)),
        sems((depth,)),
        sems((depth, 2)),
        sems((depth, 2)),
        sems((depth, 2)),
        sems((depth, 2)),
        sems((blocks, 2)),
        sems((blocks, 2)),
        sems((blocks,)),
        sems((blocks,)),
        sems((blocks,)),
        sems((blocks,)),
    ]
    held = pl.pallas_call(
        functools.partial(step_kernel, depth),
        out_shape=out_shape,
        in_specs=[hbm, vmem, hbm, hbm, hbm, vmem, hbm],
        out_specs=[vmem] * 9,
        scratch_shapes=scratch,
        compiler_params=pltpu.CompilerParams(
            collective_id=0, has_side_effects=True, vmem_limit_bytes=40 * 1024 * 1024
        ),
        cost_estimate=pl.CostEstimate(
            flops=40000 * n * rows * cols,
            bytes_accessed=5 * n * rows * cols,
            transcendentals=rows * cols,
        ),
    )(
        grad_kv.reshape(n, rows, cols),
        grad_gains.reshape(places, gain),
        kv_weight,
        kv_first,
        kv_second,
        jnp.stack([gain_weight, gain_first, gain_second]),
        average,
    )
    w, m, v, gw, gm, gv, kv, copy, avg = pl.pallas_call(
        store_kernel,
        out_shape=out_shape,
        in_specs=[vmem] * 9,
        out_specs=[hbm] * 9,
        scratch_shapes=[sems((9, 4))],
        compiler_params=pltpu.CompilerParams(
            has_side_effects=True, vmem_limit_bytes=16 * 1024 * 1024
        ),
    )(*held)
    return (
        w,
        m,
        v,
        gw.reshape(gain),
        gm.reshape(gain),
        gv.reshape(gain),
        kv.reshape(n * rows, cols),
        copy.reshape(places * gain),
        avg,
    )


def fits(mesh):
    return mesh.shape["tp"] == 2 and mesh.shape["fsdp"] % 4 == 0 and mesh.shape["fsdp"] >= 16


def shards(
    grad_kv,
    grad_gains,
    kv_weight,
    kv_first,
    kv_second,
    gain_weight,
    gain_first,
    gain_second,
    average,
):
    kv_piece = lax.psum_scatter(
        grad_kv[0].astype(jnp.float32), "fsdp", scatter_dimension=0, tiled=True
    )
    kv_square = jnp.sum(kv_piece * kv_piece)
    flat_gain = grad_gains.reshape(-1).astype(jnp.float32)
    gain_piece = lax.psum_scatter(flat_gain, ("fsdp", "tp"), scatter_dimension=0, tiled=True)
    total = lax.psum(kv_square + jnp.sum(gain_piece * gain_piece), ("fsdp", "tp"))
    factor = jnp.minimum(jnp.float32(1.0), 1.0 / jnp.sqrt(total / PARAMS + 1e-06))
    kv_w, kv_m, kv_v = adam_update(kv_piece, kv_first, kv_second, kv_weight, factor, 0.1)
    gain_w, gain_m, gain_v = adam_update(
        gain_piece, gain_first, gain_second, gain_weight, factor, 0.0
    )
    gain_copy = lax.all_gather(gain_w.astype(jnp.bfloat16), ("fsdp", "tp"), axis=0, tiled=True)
    kv_rounded = kv_w.astype(jnp.bfloat16)
    kv_blocks = lax.all_gather(kv_rounded, "fsdp", axis=0, tiled=True)
    shard_count = lax.axis_size("fsdp")
    tp_count = lax.axis_size("tp")
    columns = kv_rounded.shape[1]
    row_count = kv_rounded.shape[0] // tp_count
    moved = lax.all_to_all(
        kv_blocks.reshape(shard_count, tp_count, row_count, columns),
        "tp",
        split_axis=1,
        concat_axis=3,
        tiled=True,
    )
    moved = moved.reshape(shard_count, row_count, columns * tp_count)
    blended = 0.8 * average.astype(jnp.float32) + 0.2 * moved.astype(jnp.float32)
    average_out = blended.astype(jnp.bfloat16)
    return (kv_w, kv_m, kv_v, gain_w, gain_m, gain_v, kv_blocks, gain_copy, average_out)


def solution(mesh):
    in_specs = (
        P("fsdp", None, "tp"),
        P("fsdp", "tp", None),
        P("fsdp", "tp"),
        P("fsdp", "tp"),
        P("fsdp", "tp"),
        P(("fsdp", "tp")),
        P(("fsdp", "tp")),
        P(("fsdp", "tp")),
        P(None, "tp", None),
    )
    out_specs = (
        P("fsdp", "tp"),
        P("fsdp", "tp"),
        P("fsdp", "tp"),
        P(("fsdp", "tp")),
        P(("fsdp", "tp")),
        P(("fsdp", "tp")),
        P(None, "tp"),
        P(),
        P(None, "tp", None),
    )
    body = fused_shards if fits(mesh) else shards
    return jax.shard_map(body, mesh=mesh, in_specs=in_specs, out_specs=out_specs, check_vma=False)
```

```python
import functools

import jax
import jax.numpy as jnp
from jax import lax
from jax.experimental import pallas as pl
from jax.experimental.pallas import tpu as pltpu
from jax.sharding import PartitionSpec as P

STEP = 100
PARAMS = 4202496
TILE = 32


def adam_update(grad, first, second, weight, factor, decay):
    clipped = factor * grad
    first_new = 0.9 * first + 0.1 * clipped
    second_new = 0.95 * second + 0.05 * clipped * clipped
    first_fix = 1.0 - 0.9**STEP
    second_fix = 1.0 - 0.95**STEP
    step_dir = first_new / first_fix / (jnp.sqrt(second_new / second_fix) + 1e-08)
    weight_new = weight - 0.001 * (step_dir + decay * weight)
    return (weight_new, first_new, second_new)


def step_kernel(
    depth,
    grad,
    gain_grad,
    w_in,
    m_in,
    v_in,
    gain_in,
    avg_in,
    wbuf,
    mbuf,
    vbuf,
    gw_out,
    gm_out,
    gv_out,
    kv,
    copy_out,
    avg,
    own,
    land1,
    send2,
    land2,
    send3,
    land3,
    acc,
    other,
    gsum,
    gland,
    gz,
    states,
    t1,
    t2,
    own_sem,
    load_sem,
    p1s,
    p1r,
    p2s,
    p2r,
    p3s,
    p3r,
    gs,
    gr,
    ss,
    sr,
    t1s,
    t1r,
    t2s,
    t2r,
    azs,
    azr,
    axs,
    axr,
    acs,
    acr,
    ays,
    ayr,
    aos,
    aor,
):
    f32, bf16 = jnp.float32, jnp.bfloat16
    f = lax.axis_index("fsdp")
    t = lax.axis_index("tp")
    c = lax.rem(f, 2)
    x = lax.rem(lax.div(f, 2), 2)
    z = lax.div(f, 4)
    rows, cols = acc.shape
    half = rows // 2

    def index(zz, xx, cc):
        return (zz * 2 + xx) * 2 + cc

    def flip(bit, by):
        return 1 - bit if by else bit

    def ahead(s):
        return lax.rem(z + s, depth)

    core_peer = (index(z, x, 1 - c), t)
    x_peer = (index(z, 1 - x, c), t)
    y_peer = (f, 1 - t)

    def z_peer(s):
        return (index(ahead(s), x, c), t)

    def near_peer(k):
        return (index(z, flip(x, k // 4), flip(c, (k // 2) % 2)), flip(t, k % 2))

    pending = []

    def push(src, dst, ssem, rsem, to):
        copy = pltpu.make_async_remote_copy(
            src_ref=src,
            dst_ref=dst,
            send_sem=ssem,
            recv_sem=rsem,
            device_id=to,
            device_id_type=pl.DeviceIdType.MESH,
        )
        copy.start()
        pending.append(copy.wait_send)
        return copy

    def local(src, dst, sem):
        copy = pltpu.make_async_copy(src, dst, sem)
        copy.start()
        return copy

    barrier = pltpu.get_barrier_semaphore()
    partners = [near_peer(k) for k in range(1, 8)] + [z_peer(s) for s in range(1, depth)]
    for to in partners:
        pl.semaphore_signal(barrier, inc=1, device_id=to, device_id_type=pl.DeviceIdType.MESH)

    order = [depth // 2] + [s for s in range(1, depth) if s != depth // 2] + [0]
    own_copy, hop1, hop2, hop3 = {}, {}, {}, {}
    for s in order:
        for dx in (1, 0):
            j = s * 2 + dx
            own_copy[j] = local(grad.at[index(ahead(s), flip(x, dx), c)], own.at[j], own_sem.at[j])
    pl.semaphore_wait(barrier, len(partners))

    def piece(h):
        return pl.ds(h * half, half)

    chunks = [(s, h) for s in order for h in range(2)]
    count = len(chunks)
    first_hops = []
    for i in range(count + 2):
        if i < count:
            first_hops.append((*chunks[i], 1))
        if i >= 2:
            first_hops.append((*chunks[i - 2], 0))

    def push_first(many):
        for s, h, dx in first_hops[:many]:
            j = s * 2 + dx
            hop1[j, h] = push(
                grad.at[index(ahead(s), flip(x, dx), 1 - c), piece(h)],
                land1.at[j, piece(h)],
                p1s.at[j, h],
                p1r.at[j, h],
                core_peer,
            )
        del first_hops[:many]

    push_first(4)

    place = f * 2 + t
    gsum[0] = gain_grad[...].astype(f32)
    states[place] = jnp.zeros(states.shape[1:], f32)
    states[place, 0:3, :] = gain_in[...]
    near = [y_peer, core_peer, x_peer]
    gain_hop, state_hop = {}, {}

    def gain_send(stage):
        count = 1 << stage
        span = pl.ds(place - lax.rem(place, count), count)
        if stage < 3:
            gain_hop[stage] = push(
                gsum.at[stage], gland.at[stage], gs.at[stage], gr.at[stage], near[stage]
            )
            state_hop[stage] = push(
                states.at[span], states.at[span], ss.at[stage], sr.at[stage], near[stage]
            )
        else:
            for s in range(1, depth):
                k = 2 + s
                gain_hop[k] = push(gz.at[z], gz.at[z], gs.at[k], gr.at[k], z_peer(s))
                state_hop[k] = push(states.at[span], states.at[span], ss.at[k], sr.at[k], z_peer(s))

    def gain_take(stage):
        gain_hop[stage].wait_recv()
        state_hop[stage].wait_recv()
        total = gsum[stage] + gland[stage]
        if stage < 2:
            gsum[stage + 1] = total
        else:
            gz[z] = total

    gain_send(0)

    def tiles(base, count, body, init=None):
        def step(i, carry):
            return body(pl.ds(pl.multiple_of(base + i * TILE, TILE), TILE), carry)

        return lax.fori_loop(0, count // TILE, step, init)

    def relay_x(s, h):
        j = s * 2 + 1
        if h == 0:
            own_copy[j].wait()
        hop1[j, h].wait_recv()

        def add2(r, carry):
            send2[s, r] = (own[j, r].astype(f32) + land1[j, r].astype(f32)).astype(bf16)
            return carry

        tiles(h * half, half, add2, 0)
        hop2[s, h] = push(
            send2.at[s, piece(h)], land2.at[s, piece(h)], p2s.at[s, h], p2r.at[s, h], x_peer
        )

    def relay_z(s, h):
        j = s * 2
        if h == 0:
            own_copy[j].wait()
        hop1[j, h].wait_recv()
        hop2[s, h].wait_recv()

        def add3(r, carry):
            value = own[j, r].astype(f32) + land1[j, r].astype(f32) + land2[s, r].astype(f32)
            if s:
                send3[s - 1, r] = value.astype(bf16)
            else:
                acc[r] = value
            return carry

        tiles(h * half, half, add3, 0)
        if s:
            hop3[s, h] = push(
                send3.at[s - 1, piece(h)],
                land3.at[s - 1, piece(h)],
                p3s.at[s - 1, h],
                p3r.at[s - 1, h],
                z_peer(s),
            )

    for i in range(count + 2):
        if i < count:
            relay_x(*chunks[i])
        push_first(2)
        if i == 1:
            loads = [
                local(w_in, wbuf, load_sem.at[0]),
                local(m_in, mbuf, load_sem.at[1]),
                local(v_in, vbuf, load_sem.at[2]),
                local(avg_in, avg, load_sem.at[3]),
            ]
        if i >= 2:
            relay_z(*chunks[i - 2])
        if i in (1, 3, 5):
            gain_take(i // 2)
            gain_send(i // 2 + 1)

    square = jnp.zeros((8, cols), f32)
    for h in range(2):
        for s in order[:-1]:
            hop3[s, h].wait_recv()

        def add4(r, carry):
            value = acc[r]
            for s in range(1, depth):
                value = value + land3[s - 1, r].astype(f32)
            acc[r] = value
            sq = value * value
            for i in range(TILE // 8):
                carry = carry + sq[i * 8 : i * 8 + 8]
            return carry

        square = tiles(h * half, half, add4, square)
    folded = square[:, 0:128]
    for i in range(1, cols // 128):
        folded = folded + square[:, i * 128 : i * 128 + 128]
    seat = (x * 2 + c) * 2 + t
    t1[seat] = folded
    sums = {}
    for k in range(1, 8):
        sums[k] = push(t1.at[seat], t1.at[seat], t1s.at[k], t1r.at[k], near_peer(k))

    for s in range(1, depth):
        gain_hop[2 + s].wait_recv()
        state_hop[2 + s].wait_recv()
    g_gain = gz[0]
    for i in range(1, depth):
        g_gain = g_gain + gz[i]
    gsum[3] = g_gain

    for copy in loads[:3]:
        copy.wait()
    for k in range(1, 8):
        sums[k].wait_recv()
    t2[z] = jnp.sum(t1[...], axis=0)
    far = {}
    for s in range(1, depth):
        far[s] = push(t2.at[z], t2.at[z], t2s.at[s], t2r.at[s], z_peer(s))
    gain_total = jnp.sum(g_gain * g_gain, keepdims=True)
    for s in range(1, depth):
        far[s].wait_recv()
    total = jnp.sum(jnp.sum(t2[...], axis=0), keepdims=True) + gain_total
    factor = jnp.minimum(f32(1.0), 1.0 / jnp.sqrt(total / PARAMS + 1e-06))

    def update(r, carry):
        new = adam_update(acc[r], mbuf[r], vbuf[r], wbuf[r], factor, 0.1)
        wbuf[r], mbuf[r], vbuf[r] = new
        kv[f, r] = new[0].astype(bf16)
        return carry


    quarter = rows // 2
    keep = pl.multiple_of(t * quarter, quarter)
    spans = [
        pl.ds(pl.multiple_of((1 - t) * quarter, quarter), quarter),
        pl.ds(keep, quarter),
    ]
    mine = pl.ds(pl.multiple_of(t * cols, cols), cols)
    theirs = pl.ds(pl.multiple_of((1 - t) * cols, cols), cols)
    def nearest(zz):
        return sorted((k for k in range(depth) if k != zz), key=lambda k: abs(k - zz))

    def source(q):
        if q == 0:
            return z
        found = jnp.int32(nearest(0)[q - 1])
        for zz in range(1, depth):
            found = jnp.where(z == zz, jnp.int32(nearest(zz)[q - 1]), found)
        return found

    sources = [source(q) for q in range(depth)]
    xlist = [(q, h) for q in range(depth) for h in range(2)]
    xhop, chop, yhop, ohop = {}, {}, {}, {}
    maybe = []

    def z_copy(q, h, slot, target):
        part = kv.at[index(sources[q], x, c), spans[h]]
        return pltpu.make_async_remote_copy(
            src_ref=part,
            dst_ref=part,
            send_sem=azs.at[slot, h],
            recv_sem=azr.at[sources[q], h],
            device_id=(index(target, x, c), t),
            device_id_type=pl.DeviceIdType.MESH,
        )

    def z_send(q, h, slot, target, on):
        copy = z_copy(q, h, slot, target)
        pl.when(on)(copy.start)
        maybe.append((on, copy.wait_send))

    def z_own(h):
        z_send(0, h, 0, z + 1, z < depth - 1)
        z_send(0, h, depth, z - 1, z > 0)

    def z_pass(q, h):
        src = sources[q]
        step = jnp.where(src < z, 1, -1)
        target = z + step
        z_copy(q, h, q, z + step).wait_recv()
        z_send(q, h, q, target, (target >= 0) & (target < depth))

    def spread(s, dx, h):
        j = s * 2 + dx
        b = index(sources[s], flip(x, dx), c)
        part = kv.at[b, spans[h]]
        if dx == 0:
            xhop[s, h] = push(part, part, axs.at[s, h], axr.at[s, h], x_peer)
        if h == 0:
            yhop[j] = push(part, other.at[b], ays.at[j], ayr.at[j], y_peer)
        chop[j, h] = push(part, part, acs.at[j, h], acr.at[j, h], core_peer)

    def blend(b):
        def body(r, carry):
            source = pl.ds(pl.multiple_of(keep + r.start, TILE), TILE)
            old = avg[b, r, mine].astype(f32)
            avg[b, r, mine] = (0.8 * old + 0.2 * kv[b, source].astype(f32)).astype(bf16)
            old = avg[b, r, theirs].astype(f32)
            avg[b, r, theirs] = (0.8 * old + 0.2 * other[b, r].astype(f32)).astype(bf16)
            return carry

        tiles(0, quarter, body, 0)

    def finish_here(s, dx):
        j = s * 2 + dx
        b = index(sources[s], flip(x, dx), c)
        yhop[j].wait_recv()
        ohop[j] = push(other.at[b], other.at[b], aos.at[j], aor.at[j], core_peer)
        blend(b)

    def finish_there(s, dx):
        j = s * 2 + dx
        b = index(sources[s], flip(x, dx), 1 - c)
        for h in range(2):
            chop[j, h].wait_recv()
        ohop[j].wait_recv()
        blend(b)

    here, there = [], []
    for i in range(len(xlist) + 5):
        if i < len(xlist):
            s, h = xlist[i]
            if s:
                z_pass(s, h)
            else:
                tiles(pl.multiple_of((1 - t if h == 0 else t) * quarter, quarter), quarter, update, 0)
                z_own(h)
            spread(s, 0, h)
            if h:
                here.append((i + 2, s, 0))
        if 2 <= i < len(xlist) + 2:
            s, h = xlist[i - 2]
            xhop[s, h].wait_recv()
            spread(s, 1, h)
            if h:
                here.append((i + 1, s, 1))
        if i == 0:
            fresh = adam_update(
                gsum[3], states[:, 1, :], states[:, 2, :], states[:, 0, :], factor, 0.0
            )
            copy_out[...] = fresh[0].astype(bf16)
            piece_grad = gsum[3, pl.ds(place, 1), :]
            gw_out[...], gm_out[...], gv_out[...] = adam_update(
                piece_grad, gain_in[1:2], gain_in[2:3], gain_in[0:1], factor, 0.0
            )
            loads[3].wait()
        for due, s, dx in here:
            if due == i:
                finish_here(s, dx)
                there.append((i + 1, s, dx))
        for due, s, dx in there:
            if due == i:
                finish_there(s, dx)
    for on, wait in maybe:
        pl.when(on)(wait)
    for wait in pending:
        wait()


def store_kernel(*refs):
    count = len(refs) // 2
    sources, targets, sem = refs[:count], refs[count:-1], refs[-1]
    copies = []
    for at, (src, dst) in enumerate(zip(sources, targets)):
        parts = 4 if src.ndim == 3 else 1
        step = src.shape[0] // parts
        for part in range(parts):
            span = pl.ds(part * step, step)
            copy = pltpu.make_async_copy(src.at[span], dst.at[span], sem.at[at, part])
            copy.start()
            copies.append(copy)
    for copy in copies:
        copy.wait()


def fused_shards(
    grad_kv,
    grad_gains,
    kv_weight,
    kv_first,
    kv_second,
    gain_weight,
    gain_first,
    gain_second,
    average,
):
    n = lax.axis_size("fsdp")
    places = n * lax.axis_size("tp")
    depth = n // 4
    rows, cols = kv_weight.shape
    gain = gain_weight.shape[0]
    f32, bf16 = jnp.float32, jnp.bfloat16
    vmem, hbm = pl.BlockSpec(memory_space=pltpu.VMEM), pl.BlockSpec(memory_space=pltpu.HBM)
    sems = pltpu.SemaphoreType.DMA
    blocks = 2 * depth
    out_shape = [
        jax.ShapeDtypeStruct((rows, cols), f32),
        jax.ShapeDtypeStruct((rows, cols), f32),
        jax.ShapeDtypeStruct((rows, cols), f32),
        jax.ShapeDtypeStruct((1, gain), f32),
        jax.ShapeDtypeStruct((1, gain), f32),
        jax.ShapeDtypeStruct((1, gain), f32),
        jax.ShapeDtypeStruct((n, rows, cols), bf16),
        jax.ShapeDtypeStruct((places, gain), bf16),
        jax.ShapeDtypeStruct(average.shape, bf16),
    ]
    scratch = [
        pltpu.VMEM((blocks, rows, cols), bf16),
        pltpu.VMEM((blocks, rows, cols), bf16),
        pltpu.VMEM((depth, rows, cols), bf16),
        pltpu.VMEM((depth, rows, cols), bf16),
        pltpu.VMEM((depth - 1, rows, cols), bf16),
        pltpu.VMEM((depth - 1, rows, cols), bf16),
        pltpu.VMEM((rows, cols), f32),
        pltpu.VMEM((n, rows // 2, cols), bf16),
        pltpu.VMEM((4, places, gain), f32),
        pltpu.VMEM((3, places, gain), f32),
        pltpu.VMEM((depth, places, gain), f32),
        pltpu.VMEM((places, 8, gain), f32),
        pltpu.VMEM((8, 8, 128), f32),
        pltpu.VMEM((depth, 8, 128), f32),
        sems((blocks,)),
        sems((4,)),
        sems((blocks, 2)),
        sems((blocks, 2)),
        sems((depth, 2)),
        sems((depth, 2)),
        sems((depth - 1, 2)),
        sems((depth - 1, 2)),
        sems((depth + 2,)),
        sems((depth + 2,)),
        sems((depth + 2,)),
        sems((depth + 2,)),
        sems((8,)),
        sems((8,)),
        sems((depth,)),
        sems((depth,)),
        sems((depth + 1, 2)),
        sems((depth, 2)),
        sems((depth, 2)),
        sems((depth, 2)),
        sems((blocks, 2)),
        sems((blocks, 2)),
        sems((blocks,)),
        sems((blocks,)),
        sems((blocks,)),
        sems((blocks,)),
    ]
    held = pl.pallas_call(
        functools.partial(step_kernel, depth),
        out_shape=out_shape,
        in_specs=[hbm, vmem, hbm, hbm, hbm, vmem, hbm],
        out_specs=[vmem] * 9,
        scratch_shapes=scratch,
        compiler_params=pltpu.CompilerParams(
            collective_id=0, has_side_effects=True, vmem_limit_bytes=40 * 1024 * 1024
        ),
        cost_estimate=pl.CostEstimate(
            flops=40000 * n * rows * cols,
            bytes_accessed=5 * n * rows * cols,
            transcendentals=rows * cols,
        ),
    )(
        grad_kv.reshape(n, rows, cols),
        grad_gains.reshape(places, gain),
        kv_weight,
        kv_first,
        kv_second,
        jnp.stack([gain_weight, gain_first, gain_second]),
        average,
    )
    w, m, v, gw, gm, gv, kv, copy, avg = pl.pallas_call(
        store_kernel,
        out_shape=out_shape,
        in_specs=[vmem] * 9,
        out_specs=[hbm] * 9,
        scratch_shapes=[sems((9, 4))],
        compiler_params=pltpu.CompilerParams(
            has_side_effects=True, vmem_limit_bytes=16 * 1024 * 1024
        ),
    )(*held)
    return (
        w,
        m,
        v,
        gw.reshape(gain),
        gm.reshape(gain),
        gv.reshape(gain),
        kv.reshape(n * rows, cols),
        copy.reshape(places * gain),
        avg,
    )


def fits(mesh):
    return mesh.shape["tp"] == 2 and mesh.shape["fsdp"] % 4 == 0 and mesh.shape["fsdp"] >= 16


def shards(
    grad_kv,
    grad_gains,
    kv_weight,
    kv_first,
    kv_second,
    gain_weight,
    gain_first,
    gain_second,
    average,
):
    kv_piece = lax.psum_scatter(
        grad_kv[0].astype(jnp.float32), "fsdp", scatter_dimension=0, tiled=True
    )
    kv_square = jnp.sum(kv_piece * kv_piece)
    flat_gain = grad_gains.reshape(-1).astype(jnp.float32)
    gain_piece = lax.psum_scatter(flat_gain, ("fsdp", "tp"), scatter_dimension=0, tiled=True)
    total = lax.psum(kv_square + jnp.sum(gain_piece * gain_piece), ("fsdp", "tp"))
    factor = jnp.minimum(jnp.float32(1.0), 1.0 / jnp.sqrt(total / PARAMS + 1e-06))
    kv_w, kv_m, kv_v = adam_update(kv_piece, kv_first, kv_second, kv_weight, factor, 0.1)
    gain_w, gain_m, gain_v = adam_update(
        gain_piece, gain_first, gain_second, gain_weight, factor, 0.0
    )
    gain_copy = lax.all_gather(gain_w.astype(jnp.bfloat16), ("fsdp", "tp"), axis=0, tiled=True)
    kv_rounded = kv_w.astype(jnp.bfloat16)
    kv_blocks = lax.all_gather(kv_rounded, "fsdp", axis=0, tiled=True)
    shard_count = lax.axis_size("fsdp")
    tp_count = lax.axis_size("tp")
    columns = kv_rounded.shape[1]
    row_count = kv_rounded.shape[0] // tp_count
    moved = lax.all_to_all(
        kv_blocks.reshape(shard_count, tp_count, row_count, columns),
        "tp",
        split_axis=1,
        concat_axis=3,
        tiled=True,
    )
    moved = moved.reshape(shard_count, row_count, columns * tp_count)
    blended = 0.8 * average.astype(jnp.float32) + 0.2 * moved.astype(jnp.float32)
    average_out = blended.astype(jnp.bfloat16)
    return (kv_w, kv_m, kv_v, gain_w, gain_m, gain_v, kv_blocks, gain_copy, average_out)


def solution(mesh):
    in_specs = (
        P("fsdp", None, "tp"),
        P("fsdp", "tp", None),
        P("fsdp", "tp"),
        P("fsdp", "tp"),
        P("fsdp", "tp"),
        P(("fsdp", "tp")),
        P(("fsdp", "tp")),
        P(("fsdp", "tp")),
        P(None, "tp", None),
    )
    out_specs = (
        P("fsdp", "tp"),
        P("fsdp", "tp"),
        P("fsdp", "tp"),
        P(("fsdp", "tp")),
        P(("fsdp", "tp")),
        P(("fsdp", "tp")),
        P(None, "tp"),
        P(),
        P(None, "tp", None),
    )
    body = fused_shards if fits(mesh) else shards
    return jax.shard_map(body, mesh=mesh, in_specs=in_specs, out_specs=out_specs, check_vma=False)
```

```python
import functools

import jax
import jax.numpy as jnp
from jax import lax
from jax.experimental import pallas as pl
from jax.experimental.pallas import tpu as pltpu
from jax.sharding import PartitionSpec as P

STEP = 100
PARAMS = 4202496
TILE = 64


def adam_update(grad, first, second, weight, factor, decay):
    clipped = factor * grad
    first_new = 0.9 * first + 0.1 * clipped
    second_new = 0.95 * second + 0.05 * clipped * clipped
    first_fix = 1.0 - 0.9**STEP
    second_fix = 1.0 - 0.95**STEP
    step_dir = first_new / first_fix / (jnp.sqrt(second_new / second_fix) + 1e-08)
    weight_new = weight - 0.001 * (step_dir + decay * weight)
    return (weight_new, first_new, second_new)


def step_kernel(
    depth,
    grad,
    gain_grad,
    state_in,
    gain_in,
    avg_in,
    wbuf,
    mbuf,
    vbuf,
    gw_out,
    gm_out,
    gv_out,
    kv,
    copy_out,
    avg,
    own,
    land1,
    send2,
    land2,
    send3,
    land3,
    acc,
    other,
    gsum,
    gland,
    gz,
    states,
    t1,
    t2,
    own_sem,
    load_sem,
    p1s,
    p1r,
    p2s,
    p2r,
    p3s,
    p3r,
    gs,
    gr,
    ss,
    sr,
    t1s,
    t1r,
    t2s,
    t2r,
    azs,
    azr,
    axs,
    axr,
    acs,
    acr,
    ays,
    ayr,
    aos,
    aor,
):
    f32, bf16 = jnp.float32, jnp.bfloat16
    f = lax.axis_index("fsdp")
    t = lax.axis_index("tp")
    c = lax.rem(f, 2)
    x = lax.rem(lax.div(f, 2), 2)
    z = lax.div(f, 4)
    rows, cols = acc.shape
    half = rows // 2

    def index(zz, xx, cc):
        return (zz * 2 + xx) * 2 + cc

    def flip(bit, by):
        return 1 - bit if by else bit

    def ahead(s):
        return lax.rem(z + s, depth)

    core_peer = (index(z, x, 1 - c), t)
    x_peer = (index(z, 1 - x, c), t)
    y_peer = (f, 1 - t)

    def z_peer(s):
        return (index(ahead(s), x, c), t)

    def near_peer(k):
        return (index(z, flip(x, k // 4), flip(c, (k // 2) % 2)), flip(t, k % 2))

    pending = []

    def push(src, dst, ssem, rsem, to):
        copy = pltpu.make_async_remote_copy(
            src_ref=src,
            dst_ref=dst,
            send_sem=ssem,
            recv_sem=rsem,
            device_id=to,
            device_id_type=pl.DeviceIdType.MESH,
        )
        copy.start()
        pending.append(copy.wait_send)
        return copy

    def local(src, dst, sem):
        copy = pltpu.make_async_copy(src, dst, sem)
        copy.start()
        return copy

    barrier = pltpu.get_barrier_semaphore()
    partners = [near_peer(k) for k in range(1, 8)] + [z_peer(s) for s in range(1, depth)]
    for to in partners:
        pl.semaphore_signal(barrier, inc=1, device_id=to, device_id_type=pl.DeviceIdType.MESH)

    order = [depth // 2] + [s for s in range(1, depth) if s != depth // 2] + [0]
    own_copy, hop1, hop2, hop3 = {}, {}, {}, {}
    for s in order:
        for dx in (1, 0):
            j = s * 2 + dx
            own_copy[j] = local(grad.at[index(ahead(s), flip(x, dx), c)], own.at[j], own_sem.at[j])
    pl.semaphore_wait(barrier, len(partners))

    def piece(h):
        return pl.ds(h * half, half)

    chunks = [(s, h) for s in order for h in range(2)]
    count = len(chunks)
    first_hops = []
    for i in range(count + 2):
        if i < count:
            first_hops.append((*chunks[i], 1))
        if i >= 2:
            first_hops.append((*chunks[i - 2], 0))

    def push_first(many):
        for s, h, dx in first_hops[:many]:
            j = s * 2 + dx
            hop1[j, h] = push(
                grad.at[index(ahead(s), flip(x, dx), 1 - c), piece(h)],
                land1.at[j, piece(h)],
                p1s.at[j, h],
                p1r.at[j, h],
                core_peer,
            )
        del first_hops[:many]

    push_first(4)

    place = f * 2 + t
    gsum[0] = gain_grad[...].astype(f32)
    states[place] = jnp.zeros(states.shape[1:], f32)
    states[place, 0:3, :] = gain_in[...]
    near = [y_peer, core_peer, x_peer]
    gain_hop, state_hop = {}, {}

    def gain_send(stage):
        count = 1 << stage
        span = pl.ds(place - lax.rem(place, count), count)
        if stage < 3:
            gain_hop[stage] = push(
                gsum.at[stage], gland.at[stage], gs.at[stage], gr.at[stage], near[stage]
            )
            state_hop[stage] = push(
                states.at[span], states.at[span], ss.at[stage], sr.at[stage], near[stage]
            )
        else:
            for s in range(1, depth):
                k = 2 + s
                gain_hop[k] = push(gz.at[z], gz.at[z], gs.at[k], gr.at[k], z_peer(s))
                state_hop[k] = push(states.at[span], states.at[span], ss.at[k], sr.at[k], z_peer(s))

    def gain_take(stage):
        gain_hop[stage].wait_recv()
        state_hop[stage].wait_recv()
        total = gsum[stage] + gland[stage]
        if stage < 2:
            gsum[stage + 1] = total
        else:
            gz[z] = total

    gain_send(0)

    def tiles(base, count, body, init=None):
        def step(i, carry):
            return body(pl.ds(pl.multiple_of(base + i * TILE, TILE), TILE), carry)

        return lax.fori_loop(0, count // TILE, step, init)

    def relay_x(s, h):
        j = s * 2 + 1
        if h == 0:
            own_copy[j].wait()
        hop1[j, h].wait_recv()

        def add2(r, carry):
            send2[s, r] = (own[j, r].astype(f32) + land1[j, r].astype(f32)).astype(bf16)
            return carry

        tiles(h * half, half, add2, 0)
        hop2[s, h] = push(
            send2.at[s, piece(h)], land2.at[s, piece(h)], p2s.at[s, h], p2r.at[s, h], x_peer
        )

    def relay_z(s, h):
        j = s * 2
        if h == 0:
            own_copy[j].wait()
        hop1[j, h].wait_recv()
        hop2[s, h].wait_recv()

        def add3(r, carry):
            value = own[j, r].astype(f32) + land1[j, r].astype(f32) + land2[s, r].astype(f32)
            if s:
                send3[s - 1, r] = value.astype(bf16)
            else:
                acc[r] = value
            return carry

        tiles(h * half, half, add3, 0)
        if s:
            hop3[s, h] = push(
                send3.at[s - 1, piece(h)],
                land3.at[s - 1, piece(h)],
                p3s.at[s - 1, h],
                p3r.at[s - 1, h],
                z_peer(s),
            )

    for i in range(count + 2):
        if i < count:
            relay_x(*chunks[i])
        push_first(2)
        if i == 1:
            loads = [
                local(avg_in, avg, load_sem.at[0]),
            ]
        if i >= 2:
            relay_z(*chunks[i - 2])
        if i in (1, 3, 5):
            gain_take(i // 2)
            gain_send(i // 2 + 1)

    square = jnp.zeros((8, cols), f32)
    for h in range(2):
        for s in order[:-1]:
            hop3[s, h].wait_recv()

        def add4(r, carry):
            value = acc[r]
            for s in range(1, depth):
                value = value + land3[s - 1, r].astype(f32)
            acc[r] = value
            sq = value * value
            for i in range(TILE // 8):
                carry = carry + sq[i * 8 : i * 8 + 8]
            return carry

        square = tiles(h * half, half, add4, square)
    folded = square[:, 0:128]
    for i in range(1, cols // 128):
        folded = folded + square[:, i * 128 : i * 128 + 128]
    seat = (x * 2 + c) * 2 + t
    t1[seat] = folded
    sums = {}
    for k in range(1, 8):
        sums[k] = push(t1.at[seat], t1.at[seat], t1s.at[k], t1r.at[k], near_peer(k))

    for s in range(1, depth):
        gain_hop[2 + s].wait_recv()
        state_hop[2 + s].wait_recv()
    g_gain = gz[0]
    for i in range(1, depth):
        g_gain = g_gain + gz[i]
    gsum[3] = g_gain

    for k in range(1, 8):
        sums[k].wait_recv()
    t2[z] = jnp.sum(t1[...], axis=0)
    far = {}
    for s in range(1, depth):
        far[s] = push(t2.at[z], t2.at[z], t2s.at[s], t2r.at[s], z_peer(s))
    gain_total = jnp.sum(g_gain * g_gain, keepdims=True)
    for s in range(1, depth):
        far[s].wait_recv()
    total = jnp.sum(jnp.sum(t2[...], axis=0), keepdims=True) + gain_total
    factor = jnp.minimum(f32(1.0), 1.0 / jnp.sqrt(total / PARAMS + 1e-06))

    def update(r, carry):
        new = adam_update(acc[r], state_in[1, r], state_in[2, r], state_in[0, r], factor, 0.1)
        wbuf[r], mbuf[r], vbuf[r] = new
        kv[f, r] = new[0].astype(bf16)
        return carry


    quarter = rows // 2
    keep = pl.multiple_of(t * quarter, quarter)
    spans = [
        pl.ds(pl.multiple_of((1 - t) * quarter, quarter), quarter),
        pl.ds(keep, quarter),
    ]
    mine = pl.ds(pl.multiple_of(t * cols, cols), cols)
    theirs = pl.ds(pl.multiple_of((1 - t) * cols, cols), cols)
    def nearest(zz):
        return sorted((k for k in range(depth) if k != zz), key=lambda k: abs(k - zz))

    def source(q):
        if q == 0:
            return z
        found = jnp.int32(nearest(0)[q - 1])
        for zz in range(1, depth):
            found = jnp.where(z == zz, jnp.int32(nearest(zz)[q - 1]), found)
        return found

    sources = [source(q) for q in range(depth)]
    xlist = [(q, h) for q in range(depth) for h in range(2)]
    xhop, chop, yhop, ohop = {}, {}, {}, {}
    maybe = []

    def z_copy(q, h, slot, target):
        part = kv.at[index(sources[q], x, c), spans[h]]
        return pltpu.make_async_remote_copy(
            src_ref=part,
            dst_ref=part,
            send_sem=azs.at[slot, h],
            recv_sem=azr.at[sources[q], h],
            device_id=(index(target, x, c), t),
            device_id_type=pl.DeviceIdType.MESH,
        )

    def z_send(q, h, slot, target, on):
        copy = z_copy(q, h, slot, target)
        pl.when(on)(copy.start)
        maybe.append((on, copy.wait_send))

    def z_own(h):
        z_send(0, h, 0, z + 1, z < depth - 1)
        z_send(0, h, depth, z - 1, z > 0)

    def z_pass(q, h):
        src = sources[q]
        step = jnp.where(src < z, 1, -1)
        target = z + step
        z_copy(q, h, q, z + step).wait_recv()
        z_send(q, h, q, target, (target >= 0) & (target < depth))

    def spread(s, dx, h):
        j = s * 2 + dx
        b = index(sources[s], flip(x, dx), c)
        part = kv.at[b, spans[h]]
        if dx == 0:
            xhop[s, h] = push(part, part, axs.at[s, h], axr.at[s, h], x_peer)
        if h == 0:
            yhop[j] = push(part, other.at[b], ays.at[j], ayr.at[j], y_peer)
        chop[j, h] = push(part, part, acs.at[j, h], acr.at[j, h], core_peer)

    def blend(b):
        def body(r, carry):
            source = pl.ds(pl.multiple_of(keep + r.start, TILE), TILE)
            old = avg[b, r, mine].astype(f32)
            avg[b, r, mine] = (0.8 * old + 0.2 * kv[b, source].astype(f32)).astype(bf16)
            old = avg[b, r, theirs].astype(f32)
            avg[b, r, theirs] = (0.8 * old + 0.2 * other[b, r].astype(f32)).astype(bf16)
            return carry

        tiles(0, quarter, body, 0)

    def finish_here(s, dx):
        j = s * 2 + dx
        b = index(sources[s], flip(x, dx), c)
        yhop[j].wait_recv()
        ohop[j] = push(other.at[b], other.at[b], aos.at[j], aor.at[j], core_peer)
        blend(b)

    def finish_there(s, dx):
        j = s * 2 + dx
        b = index(sources[s], flip(x, dx), 1 - c)
        for h in range(2):
            chop[j, h].wait_recv()
        ohop[j].wait_recv()
        blend(b)

    here, there = [], []
    for i in range(len(xlist) + 5):
        if i < len(xlist):
            s, h = xlist[i]
            if s:
                z_pass(s, h)
            else:
                tiles(pl.multiple_of((1 - t if h == 0 else t) * quarter, quarter), quarter, update, 0)
                z_own(h)
            spread(s, 0, h)
            if h:
                here.append((i + 2, s, 0))
        if 2 <= i < len(xlist) + 2:
            s, h = xlist[i - 2]
            xhop[s, h].wait_recv()
            spread(s, 1, h)
            if h:
                here.append((i + 1, s, 1))
        if i == 0:
            fresh = adam_update(
                gsum[3], states[:, 1, :], states[:, 2, :], states[:, 0, :], factor, 0.0
            )
            copy_out[...] = fresh[0].astype(bf16)
            piece_grad = gsum[3, pl.ds(place, 1), :]
            gw_out[...], gm_out[...], gv_out[...] = adam_update(
                piece_grad, gain_in[1:2], gain_in[2:3], gain_in[0:1], factor, 0.0
            )
            loads[0].wait()
        for due, s, dx in here:
            if due == i:
                finish_here(s, dx)
                there.append((i + 1, s, dx))
        for due, s, dx in there:
            if due == i:
                finish_there(s, dx)
    for on, wait in maybe:
        pl.when(on)(wait)
    for wait in pending:
        wait()


def store_kernel(*refs):
    count = len(refs) // 2
    sources, targets, sem = refs[:count], refs[count:-1], refs[-1]
    copies = []
    for at, (src, dst) in enumerate(zip(sources, targets)):
        parts = 4 if src.ndim == 3 else 1
        step = src.shape[0] // parts
        for part in range(parts):
            span = pl.ds(part * step, step)
            copy = pltpu.make_async_copy(src.at[span], dst.at[span], sem.at[at, part])
            copy.start()
            copies.append(copy)
    for copy in copies:
        copy.wait()


def fused_shards(
    grad_kv,
    grad_gains,
    kv_weight,
    kv_first,
    kv_second,
    gain_weight,
    gain_first,
    gain_second,
    average,
):
    n = lax.axis_size("fsdp")
    places = n * lax.axis_size("tp")
    depth = n // 4
    rows, cols = kv_weight.shape
    gain = gain_weight.shape[0]
    f32, bf16 = jnp.float32, jnp.bfloat16
    vmem, hbm = pl.BlockSpec(memory_space=pltpu.VMEM), pl.BlockSpec(memory_space=pltpu.HBM)
    sems = pltpu.SemaphoreType.DMA
    blocks = 2 * depth
    out_shape = [
        jax.ShapeDtypeStruct((rows, cols), f32),
        jax.ShapeDtypeStruct((rows, cols), f32),
        jax.ShapeDtypeStruct((rows, cols), f32),
        jax.ShapeDtypeStruct((1, gain), f32),
        jax.ShapeDtypeStruct((1, gain), f32),
        jax.ShapeDtypeStruct((1, gain), f32),
        jax.ShapeDtypeStruct((n, rows, cols), bf16),
        jax.ShapeDtypeStruct((places, gain), bf16),
        jax.ShapeDtypeStruct(average.shape, bf16),
    ]
    scratch = [
        pltpu.VMEM((blocks, rows, cols), bf16),
        pltpu.VMEM((blocks, rows, cols), bf16),
        pltpu.VMEM((depth, rows, cols), bf16),
        pltpu.VMEM((depth, rows, cols), bf16),
        pltpu.VMEM((depth - 1, rows, cols), bf16),
        pltpu.VMEM((depth - 1, rows, cols), bf16),
        pltpu.VMEM((rows, cols), f32),
        pltpu.VMEM((n, rows // 2, cols), bf16),
        pltpu.VMEM((4, places, gain), f32),
        pltpu.VMEM((3, places, gain), f32),
        pltpu.VMEM((depth, places, gain), f32),
        pltpu.VMEM((places, 8, gain), f32),
        pltpu.VMEM((8, 8, 128), f32),
        pltpu.VMEM((depth, 8, 128), f32),
        sems((blocks,)),
        sems((1,)),
        sems((blocks, 2)),
        sems((blocks, 2)),
        sems((depth, 2)),
        sems((depth, 2)),
        sems((depth - 1, 2)),
        sems((depth - 1, 2)),
        sems((depth + 2,)),
        sems((depth + 2,)),
        sems((depth + 2,)),
        sems((depth + 2,)),
        sems((8,)),
        sems((8,)),
        sems((depth,)),
        sems((depth,)),
        sems((depth + 1, 2)),
        sems((depth, 2)),
        sems((depth, 2)),
        sems((depth, 2)),
        sems((blocks, 2)),
        sems((blocks, 2)),
        sems((blocks,)),
        sems((blocks,)),
        sems((blocks,)),
        sems((blocks,)),
    ]
    held = pl.pallas_call(
        functools.partial(step_kernel, depth),
        out_shape=out_shape,
        in_specs=[hbm, vmem, vmem, vmem, hbm],
        out_specs=[vmem] * 9,
        scratch_shapes=scratch,
        compiler_params=pltpu.CompilerParams(
            collective_id=0, has_side_effects=True, vmem_limit_bytes=40 * 1024 * 1024
        ),
        cost_estimate=pl.CostEstimate(
            flops=40000 * n * rows * cols,
            bytes_accessed=5 * n * rows * cols,
            transcendentals=rows * cols,
        ),
    )(
        grad_kv.reshape(n, rows, cols),
        grad_gains.reshape(places, gain),
        jnp.stack([kv_weight, kv_first, kv_second]),
        jnp.stack([gain_weight, gain_first, gain_second]),
        average,
    )
    w, m, v, gw, gm, gv, kv, copy, avg = pl.pallas_call(
        store_kernel,
        out_shape=out_shape,
        in_specs=[vmem] * 9,
        out_specs=[hbm] * 9,
        scratch_shapes=[sems((9, 4))],
        compiler_params=pltpu.CompilerParams(
            has_side_effects=True, vmem_limit_bytes=16 * 1024 * 1024
        ),
    )(*held)
    return (
        w,
        m,
        v,
        gw.reshape(gain),
        gm.reshape(gain),
        gv.reshape(gain),
        kv.reshape(n * rows, cols),
        copy.reshape(places * gain),
        avg,
    )


def fits(mesh):
    return mesh.shape["tp"] == 2 and mesh.shape["fsdp"] % 4 == 0 and mesh.shape["fsdp"] >= 16


def shards(
    grad_kv,
    grad_gains,
    kv_weight,
    kv_first,
    kv_second,
    gain_weight,
    gain_first,
    gain_second,
    average,
):
    kv_piece = lax.psum_scatter(
        grad_kv[0].astype(jnp.float32), "fsdp", scatter_dimension=0, tiled=True
    )
    kv_square = jnp.sum(kv_piece * kv_piece)
    flat_gain = grad_gains.reshape(-1).astype(jnp.float32)
    gain_piece = lax.psum_scatter(flat_gain, ("fsdp", "tp"), scatter_dimension=0, tiled=True)
    total = lax.psum(kv_square + jnp.sum(gain_piece * gain_piece), ("fsdp", "tp"))
    factor = jnp.minimum(jnp.float32(1.0), 1.0 / jnp.sqrt(total / PARAMS + 1e-06))
    kv_w, kv_m, kv_v = adam_update(kv_piece, kv_first, kv_second, kv_weight, factor, 0.1)
    gain_w, gain_m, gain_v = adam_update(
        gain_piece, gain_first, gain_second, gain_weight, factor, 0.0
    )
    gain_copy = lax.all_gather(gain_w.astype(jnp.bfloat16), ("fsdp", "tp"), axis=0, tiled=True)
    kv_rounded = kv_w.astype(jnp.bfloat16)
    kv_blocks = lax.all_gather(kv_rounded, "fsdp", axis=0, tiled=True)
    shard_count = lax.axis_size("fsdp")
    tp_count = lax.axis_size("tp")
    columns = kv_rounded.shape[1]
    row_count = kv_rounded.shape[0] // tp_count
    moved = lax.all_to_all(
        kv_blocks.reshape(shard_count, tp_count, row_count, columns),
        "tp",
        split_axis=1,
        concat_axis=3,
        tiled=True,
    )
    moved = moved.reshape(shard_count, row_count, columns * tp_count)
    blended = 0.8 * average.astype(jnp.float32) + 0.2 * moved.astype(jnp.float32)
    average_out = blended.astype(jnp.bfloat16)
    return (kv_w, kv_m, kv_v, gain_w, gain_m, gain_v, kv_blocks, gain_copy, average_out)


def solution(mesh):
    in_specs = (
        P("fsdp", None, "tp"),
        P("fsdp", "tp", None),
        P("fsdp", "tp"),
        P("fsdp", "tp"),
        P("fsdp", "tp"),
        P(("fsdp", "tp")),
        P(("fsdp", "tp")),
        P(("fsdp", "tp")),
        P(None, "tp", None),
    )
    out_specs = (
        P("fsdp", "tp"),
        P("fsdp", "tp"),
        P("fsdp", "tp"),
        P(("fsdp", "tp")),
        P(("fsdp", "tp")),
        P(("fsdp", "tp")),
        P(None, "tp"),
        P(),
        P(None, "tp", None),
    )
    body = fused_shards if fits(mesh) else shards
    return jax.shard_map(body, mesh=mesh, in_specs=in_specs, out_specs=out_specs, check_vma=False)
```

```python
import functools

import jax
import jax.numpy as jnp
from jax import lax
from jax.experimental import pallas as pl
from jax.experimental.pallas import tpu as pltpu
from jax.sharding import PartitionSpec as P

STEP = 100
PARAMS = 4202496
TILE = 64


def adam_update(grad, first, second, weight, factor, decay):
    clipped = factor * grad
    first_new = 0.9 * first + 0.1 * clipped
    second_new = 0.95 * second + 0.05 * clipped * clipped
    first_fix = 1.0 - 0.9**STEP
    second_fix = 1.0 - 0.95**STEP
    step_dir = first_new / first_fix / (jnp.sqrt(second_new / second_fix) + 1e-08)
    weight_new = weight - 0.001 * (step_dir + decay * weight)
    return (weight_new, first_new, second_new)


def step_kernel(
    depth,
    grad,
    gain_grad,
    state_in,
    gain_in,
    avg_in,
    wbuf,
    mbuf,
    vbuf,
    gw_out,
    gm_out,
    gv_out,
    kv,
    copy_out,
    avg,
    own,
    land1,
    send2,
    land2,
    send3,
    land3,
    acc,
    other,
    gsum,
    gland,
    gz,
    states,
    t1,
    t2,
    own_sem,
    load_sem,
    p1s,
    p1r,
    p2s,
    p2r,
    p3s,
    p3r,
    gs,
    gr,
    ss,
    sr,
    t1s,
    t1r,
    t2s,
    t2r,
    azs,
    azr,
    axs,
    axr,
    acs,
    acr,
    ays,
    ayr,
    aos,
    aor,
):
    f32, bf16 = jnp.float32, jnp.bfloat16
    f = lax.axis_index("fsdp")
    t = lax.axis_index("tp")
    c = lax.rem(f, 2)
    x = lax.rem(lax.div(f, 2), 2)
    z = lax.div(f, 4)
    rows, cols = acc.shape
    half = rows // 2

    def index(zz, xx, cc):
        return (zz * 2 + xx) * 2 + cc

    def flip(bit, by):
        return 1 - bit if by else bit

    def ahead(s):
        return lax.rem(z + s, depth)

    core_peer = (index(z, x, 1 - c), t)
    x_peer = (index(z, 1 - x, c), t)
    y_peer = (f, 1 - t)

    def z_peer(s):
        return (index(ahead(s), x, c), t)

    def near_peer(k):
        return (index(z, flip(x, k // 4), flip(c, (k // 2) % 2)), flip(t, k % 2))

    pending = []

    def push(src, dst, ssem, rsem, to):
        copy = pltpu.make_async_remote_copy(
            src_ref=src,
            dst_ref=dst,
            send_sem=ssem,
            recv_sem=rsem,
            device_id=to,
            device_id_type=pl.DeviceIdType.MESH,
        )
        copy.start()
        pending.append(copy.wait_send)
        return copy

    def local(src, dst, sem):
        copy = pltpu.make_async_copy(src, dst, sem)
        copy.start()
        return copy

    barrier = pltpu.get_barrier_semaphore()
    partners = [near_peer(k) for k in range(1, 8)] + [z_peer(s) for s in range(1, depth)]
    for to in partners:
        pl.semaphore_signal(barrier, inc=1, device_id=to, device_id_type=pl.DeviceIdType.MESH)

    order = [depth // 2] + [s for s in range(1, depth) if s != depth // 2] + [0]
    own_copy, hop1, hop2, hop3 = {}, {}, {}, {}
    for s in order:
        for dx in (1, 0):
            j = s * 2 + dx
            own_copy[j] = local(grad.at[index(ahead(s), flip(x, dx), c)], own.at[j], own_sem.at[j])
    pl.semaphore_wait(barrier, len(partners))

    def piece(h):
        return pl.ds(h * half, half)

    chunks = [(s, h) for s in order for h in range(2)]
    count = len(chunks)
    first_hops = []
    for i in range(count + 2):
        if i < count:
            first_hops.append((*chunks[i], 1))
        if i >= 2:
            first_hops.append((*chunks[i - 2], 0))

    def push_first(many):
        for s, h, dx in first_hops[:many]:
            j = s * 2 + dx
            hop1[j, h] = push(
                grad.at[index(ahead(s), flip(x, dx), 1 - c), piece(h)],
                land1.at[j, piece(h)],
                p1s.at[j, h],
                p1r.at[j, h],
                core_peer,
            )
        del first_hops[:many]

    push_first(4)

    place = f * 2 + t
    gsum[0] = gain_grad[...].astype(f32)
    states[place] = jnp.zeros(states.shape[1:], f32)
    states[place, 0:3, :] = gain_in[...]
    near = [y_peer, core_peer, x_peer]
    gain_hop, state_hop = {}, {}

    def gain_send(stage):
        count = 1 << stage
        span = pl.ds(place - lax.rem(place, count), count)
        if stage < 3:
            gain_hop[stage] = push(
                gsum.at[stage], gland.at[stage], gs.at[stage], gr.at[stage], near[stage]
            )
            state_hop[stage] = push(
                states.at[span], states.at[span], ss.at[stage], sr.at[stage], near[stage]
            )
        else:
            for s in range(1, depth):
                k = 2 + s
                gain_hop[k] = push(gz.at[z], gz.at[z], gs.at[k], gr.at[k], z_peer(s))
                state_hop[k] = push(states.at[span], states.at[span], ss.at[k], sr.at[k], z_peer(s))

    def gain_take(stage):
        gain_hop[stage].wait_recv()
        state_hop[stage].wait_recv()
        total = gsum[stage] + gland[stage]
        if stage < 2:
            gsum[stage + 1] = total
        else:
            gz[z] = total

    gain_send(0)

    def tiles(base, count, body, init=None):
        def step(i, carry):
            return body(pl.ds(pl.multiple_of(base + i * TILE, TILE), TILE), carry)

        return lax.fori_loop(0, count // TILE, step, init)

    def relay_x(s, h):
        j = s * 2 + 1
        if h == 0:
            own_copy[j].wait()
        hop1[j, h].wait_recv()

        def add2(r, carry):
            send2[s, r] = (own[j, r].astype(f32) + land1[j, r].astype(f32)).astype(bf16)
            return carry

        tiles(h * half, half, add2, 0)
        hop2[s, h] = push(
            send2.at[s, piece(h)], land2.at[s, piece(h)], p2s.at[s, h], p2r.at[s, h], x_peer
        )

    def relay_z(s, h):
        j = s * 2
        if h == 0:
            own_copy[j].wait()
        hop1[j, h].wait_recv()
        hop2[s, h].wait_recv()

        def add3(r, carry):
            value = own[j, r].astype(f32) + land1[j, r].astype(f32) + land2[s, r].astype(f32)
            if s:
                send3[s - 1, r] = value.astype(bf16)
            else:
                acc[r] = value
            return carry

        tiles(h * half, half, add3, 0)
        if s:
            hop3[s, h] = push(
                send3.at[s - 1, piece(h)],
                land3.at[s - 1, piece(h)],
                p3s.at[s - 1, h],
                p3r.at[s - 1, h],
                z_peer(s),
            )

    for i in range(count + 2):
        if i < count:
            relay_x(*chunks[i])
        push_first(2)
        if i == 1:
            loads = [
                local(avg_in, avg, load_sem.at[0]),
            ]
        if i >= 2:
            relay_z(*chunks[i - 2])
        if i in (1, 3, 5):
            gain_take(i // 2)
            gain_send(i // 2 + 1)

    square = jnp.zeros((8, cols), f32)
    for h in range(2):
        for s in order[:-1]:
            hop3[s, h].wait_recv()

        def add4(r, carry):
            value = acc[r]
            for s in range(1, depth):
                value = value + land3[s - 1, r].astype(f32)
            acc[r] = value
            sq = value * value
            for i in range(TILE // 8):
                carry = carry + sq[i * 8 : i * 8 + 8]
            return carry

        square = tiles(h * half, half, add4, square)
    folded = square[:, 0:128]
    for i in range(1, cols // 128):
        folded = folded + square[:, i * 128 : i * 128 + 128]
    seat = (x * 2 + c) * 2 + t
    t1[seat] = folded
    sums = {}
    for k in range(1, 8):
        sums[k] = push(t1.at[seat], t1.at[seat], t1s.at[k], t1r.at[k], near_peer(k))

    for s in range(1, depth):
        gain_hop[2 + s].wait_recv()
        state_hop[2 + s].wait_recv()
    g_gain = gz[0]
    for i in range(1, depth):
        g_gain = g_gain + gz[i]
    gsum[3] = g_gain

    for k in range(1, 8):
        sums[k].wait_recv()
    t2[z] = jnp.sum(t1[...], axis=0)
    far = {}
    for s in range(1, depth):
        far[s] = push(t2.at[z], t2.at[z], t2s.at[s], t2r.at[s], z_peer(s))
    gain_total = jnp.sum(g_gain * g_gain, keepdims=True)
    for s in range(1, depth):
        far[s].wait_recv()
    total = jnp.sum(jnp.sum(t2[...], axis=0), keepdims=True) + gain_total
    factor = jnp.minimum(f32(1.0), 1.0 / jnp.sqrt(total / PARAMS + 1e-06))

    def update(r, carry):
        new = adam_update(acc[r], state_in[1, r], state_in[2, r], state_in[0, r], factor, 0.1)
        wbuf[r], mbuf[r], vbuf[r] = new
        kv[f, r] = new[0].astype(bf16)
        return carry


    quarter = rows // 2
    keep = pl.multiple_of(t * quarter, quarter)
    spans = [
        pl.ds(pl.multiple_of((1 - t) * quarter, quarter), quarter),
        pl.ds(keep, quarter),
    ]
    mine = pl.ds(pl.multiple_of(t * cols, cols), cols)
    theirs = pl.ds(pl.multiple_of((1 - t) * cols, cols), cols)
    def nearest(zz):
        return sorted((k for k in range(depth) if k != zz), key=lambda k: abs(k - zz))

    def source(q):
        if q == 0:
            return z
        found = jnp.int32(nearest(0)[q - 1])
        for zz in range(1, depth):
            found = jnp.where(z == zz, jnp.int32(nearest(zz)[q - 1]), found)
        return found

    sources = [source(q) for q in range(depth)]
    xlist = [(q, h) for q in range(depth) for h in range(2)]
    xhop, chop, yhop, ohop = {}, {}, {}, {}
    maybe = []

    def z_copy(q, h, slot, target):
        part = kv.at[index(sources[q], x, c), spans[h]]
        return pltpu.make_async_remote_copy(
            src_ref=part,
            dst_ref=part,
            send_sem=azs.at[slot, h],
            recv_sem=azr.at[sources[q], h],
            device_id=(index(target, x, c), t),
            device_id_type=pl.DeviceIdType.MESH,
        )

    def z_send(q, h, slot, target, on):
        copy = z_copy(q, h, slot, target)
        pl.when(on)(copy.start)
        maybe.append((on, copy.wait_send))

    def z_own(h):
        z_send(0, h, 0, z + 1, z < depth - 1)
        z_send(0, h, depth, z - 1, z > 0)

    def z_pass(q, h):
        src = sources[q]
        step = jnp.where(src < z, 1, -1)
        target = z + step
        z_copy(q, h, q, z + step).wait_recv()
        z_send(q, h, q, target, (target >= 0) & (target < depth))

    def spread(s, dx, h):
        j = s * 2 + dx
        b = index(sources[s], flip(x, dx), c)
        part = kv.at[b, spans[h]]
        if dx == 0:
            xhop[s, h] = push(part, part, axs.at[s, h], axr.at[s, h], x_peer)
        if h == 0:
            yhop[j] = push(part, other.at[b], ays.at[j], ayr.at[j], y_peer)
        chop[j, h] = push(part, part, acs.at[j, h], acr.at[j, h], core_peer)

    def blend(b):
        def body(r, carry):
            source = pl.ds(pl.multiple_of(keep + r.start, TILE), TILE)
            old = avg[b, r, mine].astype(f32)
            avg[b, r, mine] = (0.8 * old + 0.2 * kv[b, source].astype(f32)).astype(bf16)
            old = avg[b, r, theirs].astype(f32)
            avg[b, r, theirs] = (0.8 * old + 0.2 * other[b, r].astype(f32)).astype(bf16)
            return carry

        tiles(0, quarter, body, 0)

    def finish_here(s, dx):
        j = s * 2 + dx
        b = index(sources[s], flip(x, dx), c)
        yhop[j].wait_recv()
        ohop[j] = push(other.at[b], other.at[b], aos.at[j], aor.at[j], core_peer)
        blend(b)

    def finish_there(s, dx):
        j = s * 2 + dx
        b = index(sources[s], flip(x, dx), 1 - c)
        for h in range(2):
            chop[j, h].wait_recv()
        ohop[j].wait_recv()
        blend(b)

    here, there = [], []
    for i in range(len(xlist) + 5):
        if 2 <= i < len(xlist) + 2:
            s, h = xlist[i - 2]
            xhop[s, h].wait_recv()
            spread(s, 1, h)
            if h:
                here.append((i + 1, s, 1))
        if i < len(xlist):
            s, h = xlist[i]
            if s:
                z_pass(s, h)
            else:
                tiles(pl.multiple_of((1 - t if h == 0 else t) * quarter, quarter), quarter, update, 0)
                z_own(h)
            spread(s, 0, h)
            if h:
                here.append((i + 2, s, 0))
        if i == 0:
            fresh = adam_update(
                gsum[3], states[:, 1, :], states[:, 2, :], states[:, 0, :], factor, 0.0
            )
            copy_out[...] = fresh[0].astype(bf16)
            piece_grad = gsum[3, pl.ds(place, 1), :]
            gw_out[...], gm_out[...], gv_out[...] = adam_update(
                piece_grad, gain_in[1:2], gain_in[2:3], gain_in[0:1], factor, 0.0
            )
            loads[0].wait()
        for due, s, dx in here:
            if due == i:
                finish_here(s, dx)
                there.append((i + 1, s, dx))
        for due, s, dx in there:
            if due == i:
                finish_there(s, dx)
    for on, wait in maybe:
        pl.when(on)(wait)
    for wait in pending:
        wait()


def store_kernel(*refs):
    count = len(refs) // 2
    sources, targets, sem = refs[:count], refs[count:-1], refs[-1]
    copies = []
    for at, (src, dst) in enumerate(zip(sources, targets)):
        parts = 4 if src.ndim == 3 else 1
        step = src.shape[0] // parts
        for part in range(parts):
            span = pl.ds(part * step, step)
            copy = pltpu.make_async_copy(src.at[span], dst.at[span], sem.at[at, part])
            copy.start()
            copies.append(copy)
    for copy in copies:
        copy.wait()


def fused_shards(
    grad_kv,
    grad_gains,
    kv_weight,
    kv_first,
    kv_second,
    gain_weight,
    gain_first,
    gain_second,
    average,
):
    n = lax.axis_size("fsdp")
    places = n * lax.axis_size("tp")
    depth = n // 4
    rows, cols = kv_weight.shape
    gain = gain_weight.shape[0]
    f32, bf16 = jnp.float32, jnp.bfloat16
    vmem, hbm = pl.BlockSpec(memory_space=pltpu.VMEM), pl.BlockSpec(memory_space=pltpu.HBM)
    sems = pltpu.SemaphoreType.DMA
    blocks = 2 * depth
    out_shape = [
        jax.ShapeDtypeStruct((rows, cols), f32),
        jax.ShapeDtypeStruct((rows, cols), f32),
        jax.ShapeDtypeStruct((rows, cols), f32),
        jax.ShapeDtypeStruct((1, gain), f32),
        jax.ShapeDtypeStruct((1, gain), f32),
        jax.ShapeDtypeStruct((1, gain), f32),
        jax.ShapeDtypeStruct((n, rows, cols), bf16),
        jax.ShapeDtypeStruct((places, gain), bf16),
        jax.ShapeDtypeStruct(average.shape, bf16),
    ]
    scratch = [
        pltpu.VMEM((blocks, rows, cols), bf16),
        pltpu.VMEM((blocks, rows, cols), bf16),
        pltpu.VMEM((depth, rows, cols), bf16),
        pltpu.VMEM((depth, rows, cols), bf16),
        pltpu.VMEM((depth - 1, rows, cols), bf16),
        pltpu.VMEM((depth - 1, rows, cols), bf16),
        pltpu.VMEM((rows, cols), f32),
        pltpu.VMEM((n, rows // 2, cols), bf16),
        pltpu.VMEM((4, places, gain), f32),
        pltpu.VMEM((3, places, gain), f32),
        pltpu.VMEM((depth, places, gain), f32),
        pltpu.VMEM((places, 8, gain), f32),
        pltpu.VMEM((8, 8, 128), f32),
        pltpu.VMEM((depth, 8, 128), f32),
        sems((blocks,)),
        sems((1,)),
        sems((blocks, 2)),
        sems((blocks, 2)),
        sems((depth, 2)),
        sems((depth, 2)),
        sems((depth - 1, 2)),
        sems((depth - 1, 2)),
        sems((depth + 2,)),
        sems((depth + 2,)),
        sems((depth + 2,)),
        sems((depth + 2,)),
        sems((8,)),
        sems((8,)),
        sems((depth,)),
        sems((depth,)),
        sems((depth + 1, 2)),
        sems((depth, 2)),
        sems((depth, 2)),
        sems((depth, 2)),
        sems((blocks, 2)),
        sems((blocks, 2)),
        sems((blocks,)),
        sems((blocks,)),
        sems((blocks,)),
        sems((blocks,)),
    ]
    held = pl.pallas_call(
        functools.partial(step_kernel, depth),
        out_shape=out_shape,
        in_specs=[hbm, vmem, vmem, vmem, hbm],
        out_specs=[vmem] * 9,
        scratch_shapes=scratch,
        compiler_params=pltpu.CompilerParams(
            collective_id=0, has_side_effects=True, vmem_limit_bytes=40 * 1024 * 1024
        ),
        cost_estimate=pl.CostEstimate(
            flops=40000 * n * rows * cols,
            bytes_accessed=5 * n * rows * cols,
            transcendentals=rows * cols,
        ),
    )(
        grad_kv.reshape(n, rows, cols),
        grad_gains.reshape(places, gain),
        jnp.stack([kv_weight, kv_first, kv_second]),
        jnp.stack([gain_weight, gain_first, gain_second]),
        average,
    )
    w, m, v, gw, gm, gv, kv, copy, avg = pl.pallas_call(
        store_kernel,
        out_shape=out_shape,
        in_specs=[vmem] * 9,
        out_specs=[hbm] * 9,
        scratch_shapes=[sems((9, 4))],
        compiler_params=pltpu.CompilerParams(
            has_side_effects=True, vmem_limit_bytes=16 * 1024 * 1024
        ),
    )(*held)
    return (
        w,
        m,
        v,
        gw.reshape(gain),
        gm.reshape(gain),
        gv.reshape(gain),
        kv.reshape(n * rows, cols),
        copy.reshape(places * gain),
        avg,
    )


def fits(mesh):
    return mesh.shape["tp"] == 2 and mesh.shape["fsdp"] % 4 == 0 and mesh.shape["fsdp"] >= 16


def shards(
    grad_kv,
    grad_gains,
    kv_weight,
    kv_first,
    kv_second,
    gain_weight,
    gain_first,
    gain_second,
    average,
):
    kv_piece = lax.psum_scatter(
        grad_kv[0].astype(jnp.float32), "fsdp", scatter_dimension=0, tiled=True
    )
    kv_square = jnp.sum(kv_piece * kv_piece)
    flat_gain = grad_gains.reshape(-1).astype(jnp.float32)
    gain_piece = lax.psum_scatter(flat_gain, ("fsdp", "tp"), scatter_dimension=0, tiled=True)
    total = lax.psum(kv_square + jnp.sum(gain_piece * gain_piece), ("fsdp", "tp"))
    factor = jnp.minimum(jnp.float32(1.0), 1.0 / jnp.sqrt(total / PARAMS + 1e-06))
    kv_w, kv_m, kv_v = adam_update(kv_piece, kv_first, kv_second, kv_weight, factor, 0.1)
    gain_w, gain_m, gain_v = adam_update(
        gain_piece, gain_first, gain_second, gain_weight, factor, 0.0
    )
    gain_copy = lax.all_gather(gain_w.astype(jnp.bfloat16), ("fsdp", "tp"), axis=0, tiled=True)
    kv_rounded = kv_w.astype(jnp.bfloat16)
    kv_blocks = lax.all_gather(kv_rounded, "fsdp", axis=0, tiled=True)
    shard_count = lax.axis_size("fsdp")
    tp_count = lax.axis_size("tp")
    columns = kv_rounded.shape[1]
    row_count = kv_rounded.shape[0] // tp_count
    moved = lax.all_to_all(
        kv_blocks.reshape(shard_count, tp_count, row_count, columns),
        "tp",
        split_axis=1,
        concat_axis=3,
        tiled=True,
    )
    moved = moved.reshape(shard_count, row_count, columns * tp_count)
    blended = 0.8 * average.astype(jnp.float32) + 0.2 * moved.astype(jnp.float32)
    average_out = blended.astype(jnp.bfloat16)
    return (kv_w, kv_m, kv_v, gain_w, gain_m, gain_v, kv_blocks, gain_copy, average_out)


def solution(mesh):
    in_specs = (
        P("fsdp", None, "tp"),
        P("fsdp", "tp", None),
        P("fsdp", "tp"),
        P("fsdp", "tp"),
        P("fsdp", "tp"),
        P(("fsdp", "tp")),
        P(("fsdp", "tp")),
        P(("fsdp", "tp")),
        P(None, "tp", None),
    )
    out_specs = (
        P("fsdp", "tp"),
        P("fsdp", "tp"),
        P("fsdp", "tp"),
        P(("fsdp", "tp")),
        P(("fsdp", "tp")),
        P(("fsdp", "tp")),
        P(None, "tp"),
        P(),
        P(None, "tp", None),
    )
    body = fused_shards if fits(mesh) else shards
    return jax.shard_map(body, mesh=mesh, in_specs=in_specs, out_specs=out_specs, check_vma=False)
```
